32 devices in a mesh: dist: 8 (over z, y), rows: 4 (over x, core).
Axes of the slice: x: 2, y: 2, z: 4, core: 2. Of those that a mesh axis runs over, the one named last changes fastest.
Arguments:
- wave: float32 [8, 2, 2048, 2048], P('dist', None, 'rows'), may hold values from -6 to 6
- object_slice: float32 [2, 2048, 2048], P(None, 'rows', 'dist'), may hold values from 0 to 1.5
- fresnel: float32 [8], P('dist'), may hold values from 256 to 1024
Outputs:
- detected: float32 [8, 2, 2048, 2048], P('dist', None, 'rows')
The draws below stay inside these ranges and needn't reach their ends.
All inputs are finite; a program needn't handle non-finite values.
Results may differ from the reference program's by a relative error of at most 0.00035.
Values sent between devices are 32-bit elements; how exact they have to be, the bound alone decides.
No kernel may reach another device: no remote copies, remote signals or barrier semaphores. Data moves between devices by JAX's collectives and lax.ppermute only.
A program may use at most 128 MiB of HBM per device.

```python
import math
import jax
import jax.numpy as jnp
from jax import lax

N = 2048
DIST = 8


def steps_of(stream_key, dims, split, low, top_value):
    loudness = 1.0
    for dim, shards_of in split:
        draws = jax.random.uniform(jax.random.fold_in(jax.random.fold_in(stream_key, 6), dim), (shards_of,), jnp.float32, low / len(split), top_value / len(split))
        loudness = loudness * jnp.repeat(jnp.exp(draws), dims[dim] // shards_of).reshape((-1,) + (1,) * (len(dims) - 1 - dim))
    return loudness


def scatter_about(own_key, extent, deviation, limit, shards=(), held_as=jnp.bfloat16):
    drawn = jax.random.normal(own_key, extent, jnp.float32) * deviation
    if len(shards) > 0:
        drawn = steps_of(own_key, extent, shards, -0.22, 0.18) * drawn
    return jnp.clip(drawn, min=-limit, max=limit).astype(held_as)


def setup_inputs(seed: int = 0) -> dict:
    splits = jax.random.split(jax.random.key(seed), 4)
    return {
        "wave": scatter_about(splits[0], (DIST, 2, N, N), 1.0, 6.0, ((0, 8), (2, 4)), jnp.float32),
        "object_slice": jnp.clip(1.5 * jax.random.uniform(splits[1], (2, N, N), jnp.float32) ** steps_of(splits[1], (2, N, N), ((1, 4), (2, 8)), -0.2, 0.2), 0.0, 1.5),
        "fresnel": jnp.clip(jnp.exp(math.log(1024.0) - 1.3862944 * jax.random.uniform(splits[2], (DIST,), jnp.float32) ** steps_of(splits[2], (DIST,), ((0, 8),), -0.2, 0.2)), 256.0, 1024.0),
    }


def reference(wave, object_slice, fresnel):
    amplitude = jnp.exp(-object_slice[1])
    trans_re = amplitude * jnp.cos(object_slice[0])
    trans_im = amplitude * jnp.sin(object_slice[0])
    index_line = jnp.arange(N).astype(jnp.int32)
    frequency = jnp.where(index_line < N // 2, index_line, index_line - N).astype(jnp.float32) / N
    freq_sum = frequency[:, None] ** 2 + frequency[None, :] ** 2

    def propagate(inputs):
        field, number = inputs
        exit_re = field[0] * trans_re - field[1] * trans_im
        exit_im = field[0] * trans_im + field[1] * trans_re
        spectrum = jnp.fft.fft2(exit_re + 1j * exit_im)
        phase_angle = (-math.pi * number) * freq_sum
        spectrum = spectrum * (jnp.cos(phase_angle) + 1j * jnp.sin(phase_angle))
        result = jnp.fft.ifft2(spectrum)
        return jnp.stack((jnp.real(result), jnp.imag(result))).astype(jnp.float32)

    return lax.map(propagate, (wave, fresnel))
```

```python
import functools
import math

import jax
import jax.numpy as jnp
import numpy as np
from jax import lax
from jax.experimental import pallas as pl
from jax.experimental.pallas import tpu as pltpu
from jax.sharding import PartitionSpec as P

f32, bf16 = jnp.float32, jnp.bfloat16
LANES = 128
RADIX = 8
STRIP = 32
MIB = 1 << 20
ROOT = math.sqrt(0.5)


def turn(z, quarter):
    re, im = z
    return ((re, im), (-im, re), (-re, -im), (im, -re))[quarter % 4]


def plus(a, b):
    return (a[0] + b[0], a[1] + b[1])


def minus(a, b):
    return (a[0] - b[0], a[1] - b[1])


def dft4(z, sign):
    even, odd = plus(z[0], z[2]), plus(z[1], z[3])
    low, high = minus(z[0], z[2]), turn(minus(z[1], z[3]), sign)
    return [plus(even, odd), plus(low, high), minus(even, odd), minus(low, high)]


def dft8(z, sign):
    even, odd = dft4(z[0::2], sign), dft4(z[1::2], sign)
    (re1, im1), (re3, im3) = odd[1], odd[3]
    odd[1] = (ROOT * (re1 - sign * im1), ROOT * (im1 + sign * re1))
    odd[2] = turn(odd[2], sign)
    odd[3] = (-ROOT * (re3 + sign * im3), ROOT * (sign * re3 - im3))
    return [plus(a, b) for a, b in zip(even, odd)] + [minus(a, b) for a, b in zip(even, odd)]


def split(value):
    high = value.astype(bf16)
    return high, (value - high.astype(f32)).astype(bf16)


def dot3(a_high, a_low, b_high, b_low):
    dot = functools.partial(jnp.dot, preferred_element_type=f32)
    return dot(a_high, b_high) + (dot(a_high, b_low) + dot(a_low, b_high))


def blocks_kernel(response, wheel, right, twist, blocks):
    half = wheel.shape[1]
    k = pl.program_id(0)
    h_re, h_im = response[0, pl.ds(k, 1)], response[1, pl.ds(k, 1)]
    w_re, w_im = wheel[0], wheel[1]
    left = jnp.concatenate((w_re * h_re - w_im * h_im, w_re * h_im + w_im * h_re), axis=1)
    both = jnp.dot(left, right[...], precision=lax.Precision.HIGHEST, preferred_element_type=f32)
    both_re, both_im = both[:, :half], both[:, half:]
    t_re, t_im = twist[0, 0], twist[0, 1]
    high, low = split(both_re * t_re - both_im * t_im)
    blocks[0, 0, 0], blocks[0, 0, 1] = high, low
    high, low = split(both_re * t_im + both_im * t_re)
    blocks[0, 1, 0], blocks[0, 1, 1] = high, low


def circulant_blocks(fresnel, length):
    side = length // RADIX
    index = np.arange(RADIX)[:, None] + RADIX * np.arange(side)[None]
    freq = np.where(index < length // 2, index, index - length).astype(np.float32) / length
    phase = (-math.pi * fresnel[0]) * (freq * freq)
    response = jnp.stack((jnp.cos(phase), jnp.sin(phase)))
    line = np.arange(side)
    angle = 2 * np.pi / side * (line[:, None] * line[None] % side)
    wheel = np.stack((np.cos(angle), np.sin(angle))).astype(np.float32)
    scale = 1.0 / (side * RADIX)
    w_re, w_im = np.cos(angle).T * scale, np.sin(angle).T * scale
    right = np.block([[w_re, -w_im], [w_im, w_re]]).astype(np.float32)
    apart = np.arange(RADIX)[:, None, None] * (line[:, None] - line[None])
    twist = np.stack((np.cos(2 * np.pi / length * apart), np.sin(2 * np.pi / length * apart)), 1).astype(np.float32)
    whole = lambda *shape: pl.BlockSpec(shape, lambda k: (0,) * len(shape))
    return pl.pallas_call(
        blocks_kernel,
        grid=(RADIX,),
        out_shape=jax.ShapeDtypeStruct((RADIX, 2, 2, side, side), bf16),
        in_specs=[
            whole(2, RADIX, side),
            whole(2, side, side),
            whole(2 * side, 2 * side),
            pl.BlockSpec((1, 2, side, side), lambda k: (k, 0, 0, 0)),
        ],
        out_specs=pl.BlockSpec((1, 2, 2, side, side), lambda k: (k, 0, 0, 0, 0)),
        compiler_params=pltpu.CompilerParams(vmem_limit_bytes=32 * MIB),
        name="circulant_blocks",
    )(response, jnp.asarray(wheel), jnp.asarray(right), jnp.asarray(twist))


class Plan:
    def __init__(self, wave):
        self.group, self.dists = lax.axis_size("rows"), lax.axis_size("dist")
        self.rows, self.length = wave.shape[2], wave.shape[3]
        self.units = self.length // LANES
        self.high = min(self.units // self.dists, self.group)
        self.low = self.group // self.high
        self.picks = self.dists // self.low
        self.parts = 2 if self.picks % 2 == 0 else 1
        self.per_part = self.picks // self.parts
        self.strips = max(self.rows // LANES, 1)
        self.order = sorted(range(self.group), key=lambda jump: (-(jump // self.low), jump % self.low))

    def unit(self, place, dist, pick):
        other = jnp.bitwise_xor(dist, pick * self.low + place % self.low)
        return other * self.high + place // self.low


def pack_kernel(plan, wave, *refs):
    outs, (staged, ins, sems) = refs[:-3], refs[-3:]
    me, dist = lax.axis_index("rows"), lax.axis_index("dist")
    loads, stores = [], []
    for part in range(plan.parts):
        for jump in plan.order:
            for g in range(plan.per_part):
                slot = len(loads)
                unit = plan.unit(jnp.bitwise_xor(me, jump), dist, part * plan.per_part + g)
                start = pl.multiple_of(unit * LANES, LANES)
                out = outs[part * plan.group + jump].at[g]
                loads.append(pltpu.make_async_copy(wave.at[0, :, :, pl.ds(start, LANES)], staged.at[slot], ins.at[slot]))
                stores.append(pltpu.make_async_copy(staged.at[slot], out, sems.at[slot]))
    for load in loads:
        load.start()
    for load, store in zip(loads, stores):
        load.wait()
        store.start()
    for store in stores:
        store.wait()


def pack(plan, wave):
    count = plan.parts * plan.group
    outs = pl.pallas_call(
        functools.partial(pack_kernel, plan),
        out_shape=[jax.ShapeDtypeStruct((plan.per_part, 2, plan.rows, LANES), f32)] * count,
        in_specs=[pl.BlockSpec(memory_space=pl.ANY)],
        out_specs=[pl.BlockSpec(memory_space=pl.ANY)] * count,
        scratch_shapes=[
            pltpu.VMEM((plan.units, 2, plan.rows, LANES), f32),
            pltpu.SemaphoreType.DMA((plan.units,)),
            pltpu.SemaphoreType.DMA((plan.units,)),
        ],
        compiler_params=pltpu.CompilerParams(vmem_limit_bytes=16 * MIB),
        cost_estimate=pl.CostEstimate(flops=0, bytes_accessed=16 * MIB, transcendentals=0),
        name="pack",
    )(wave)
    return [outs[part * plan.group : (part + 1) * plan.group] for part in range(plan.parts)]


def transmission_kernel(*refs):
    out = refs[-1]
    for h, piece in enumerate(refs[:-1]):
        amplitude = jnp.exp(-piece[1])
        out[h, 0], out[h, 1] = amplitude * jnp.cos(piece[0]), amplitude * jnp.sin(piece[0])


def transmission(held):
    rows = held[0].shape[1]
    return pl.pallas_call(
        transmission_kernel,
        grid=(rows // STRIP,),
        out_shape=jax.ShapeDtypeStruct((len(held),) + held[0].shape, f32),
        in_specs=[pl.BlockSpec((2, STRIP, LANES), lambda s: (0, s, 0))] * len(held),
        out_specs=pl.BlockSpec((len(held), 2, STRIP, LANES), lambda s: (0, 0, s, 0)),
        name="transmission",
    )(*held)


def column_kernel(plan, counts, *refs):
    n, low = plan.group, plan.low
    waves, refs = refs[:n], refs[n:]
    slices = []
    for g in range(plan.per_part):
        slices.append([])
        for count in counts:
            slices[g].append(refs[:count])
            refs = refs[count:]
    blocks, outs = refs[0], refs[1:-4]
    field, x_high, x_low, y = refs[-4:]
    me, step = lax.axis_index("rows"), pl.program_id(0)
    rows, side = plan.rows, plan.length // RADIX
    per_out = len(outs) // n
    for g in range(plan.per_part):
        for jump in range(n):
            cases = slices[g][jump % low]

            @pl.when(step == g)
            def _(jump=jump, cases=cases):
                base = jnp.bitwise_xor(me, jump) * rows

                @pl.loop(0, rows // STRIP)
                def _(s):
                    here = pl.ds(pl.multiple_of(s * STRIP, STRIP), STRIP)
                    read = lambda c: pick(me % low, [case[jump // low, c, here] for case in cases])
                    t_re, t_im = read(0), read(1)
                    w_re, w_im = waves[jump][0, 0, here], waves[jump][0, 1, here]
                    there = pl.ds(pl.multiple_of(base + s * STRIP, STRIP), STRIP)
                    field[0, there] = w_re * t_re - w_im * t_im
                    field[1, there] = w_re * t_im + w_im * t_re

    @pl.loop(0, side // STRIP)
    def _(s):
        at = lambda b: pl.ds(pl.multiple_of(b * side + s * STRIP, STRIP), STRIP)
        here = pl.ds(pl.multiple_of(s * STRIP, STRIP), STRIP)
        for k, z in enumerate(dft8([(field[0, at(b)], field[1, at(b)]) for b in range(RADIX)], -1)):
            x_high[k, here], x_low[k, here] = split(jnp.concatenate(z, axis=1))

    @pl.loop(0, RADIX)
    def _(k):
        by_re = dot3(blocks[k, 0, 0], blocks[k, 0, 1], x_high[k], x_low[k])
        by_im = dot3(blocks[k, 1, 0], blocks[k, 1, 1], x_high[k], x_low[k])
        y[k, :, :LANES] = by_re[:, :LANES] - by_im[:, LANES:]
        y[k, :, LANES:] = by_re[:, LANES:] + by_im[:, :LANES]

    @pl.loop(0, side // STRIP)
    def _(s):
        here = pl.ds(pl.multiple_of(s * STRIP, STRIP), STRIP)
        for b, z in enumerate(dft8([(y[k, here, :LANES], y[k, here, LANES:]) for k in range(RADIX)], 1)):
            there = pl.ds(pl.multiple_of(b * side + s * STRIP, STRIP), STRIP)
            field[0, there], field[1, there] = z

    tall = rows // per_out
    for jump in range(n):
        base = jnp.bitwise_xor(me, jump) * rows
        for r in range(per_out):
            there = pl.ds(pl.multiple_of(base + r * tall, tall), tall)
            outs[jump * per_out + r][0, 0] = field[0, there]
            outs[jump * per_out + r][0, 1] = field[1, there]


def column_pass(plan, part, waves, slices, blocks):
    side = plan.length // RADIX
    per_out = plan.strips if part == plan.parts - 1 else 1
    tall = plan.rows // per_out
    flat = [array for of_pick in slices for cases in of_pick for array in cases]
    wave_spec = pl.BlockSpec((1, 2, plan.rows, LANES), lambda g: (g, 0, 0, 0))
    slice_spec = pl.BlockSpec((plan.high, 2, plan.rows, LANES), lambda g: (0, 0, 0, 0))
    out_spec = pl.BlockSpec((1, 2, tall, LANES), lambda g: (g, 0, 0, 0))
    count = plan.group * per_out
    outs = pl.pallas_call(
        functools.partial(column_kernel, plan, [len(cases) for cases in slices[0]]),
        grid=(plan.per_part,),
        out_shape=[jax.ShapeDtypeStruct((plan.per_part, 2, tall, LANES), f32)] * count,
        in_specs=[wave_spec] * plan.group
        + [slice_spec] * len(flat)
        + [pl.BlockSpec((RADIX, 2, 2, side, side), lambda g: (0, 0, 0, 0, 0))],
        out_specs=[out_spec] * count,
        scratch_shapes=[
            pltpu.VMEM((2, plan.length, LANES), f32),
            pltpu.VMEM((RADIX, side, 2 * LANES), bf16),
            pltpu.VMEM((RADIX, side, 2 * LANES), bf16),
            pltpu.VMEM((RADIX, side, 2 * LANES), f32),
        ],
        compiler_params=pltpu.CompilerParams(vmem_limit_bytes=48 * MIB),
        cost_estimate=pl.CostEstimate(flops=6 * MIB * 1024 // plan.parts, bytes_accessed=32 * MIB // plan.parts, transcendentals=0),
        name=f"column_pass_{part}",
    )(*waves, *flat, blocks)
    return [outs[jump * per_out : (jump + 1) * per_out] for jump in range(plan.group)]


def row_kernel(plan, *refs):
    n = plan.group
    ins, blocks, out = refs[: plan.parts * n], refs[plan.parts * n], refs[-5]
    field, x_high, x_low, y = refs[-4:]
    me, dist = lax.axis_index("rows"), lax.axis_index("dist")
    side, tall = plan.length // RADIX, field.shape[2]
    for part in range(plan.parts):
        for jump in range(n):
            place = jnp.bitwise_xor(me, jump)
            for g in range(plan.per_part):
                unit = plan.unit(place, dist, part * plan.per_part + g)
                field[unit] = ins[part * n + jump][g]
    wide = side // LANES

    @pl.loop(0, tall // 16)
    def _(s):
        here = pl.ds(pl.multiple_of(s * 16, 16), 16)
        line = lambda b, c: jnp.concatenate([field[b * wide + v, c, here] for v in range(wide)], axis=1)
        for k, (re, im) in enumerate(dft8([(line(b, 0), line(b, 1)) for b in range(RADIX)], -1)):
            x_high[k, 0, here], x_low[k, 0, here] = split(re)
            x_high[k, 1, here], x_low[k, 1, here] = split(im)

    @pl.loop(0, RADIX)
    def _(k):
        back = lax.rem(RADIX - k, RADIX)
        xh = x_high[k].reshape(2 * tall, side)
        xl = x_low[k].reshape(2 * tall, side)
        by_re = dot3(xh, xl, blocks[back, 0, 0], blocks[back, 0, 1])
        by_im = dot3(xh, xl, blocks[back, 1, 0], blocks[back, 1, 1])
        y[k, 0] = by_re[:tall] - by_im[tall:]
        y[k, 1] = by_re[tall:] + by_im[:tall]

    @pl.loop(0, tall // 16)
    def _(s):
        here = pl.ds(pl.multiple_of(s * 16, 16), 16)
        for b, (re, im) in enumerate(dft8([(y[k, 0, here], y[k, 1, here]) for k in range(RADIX)], 1)):
            out[0, 0, here, b * side : (b + 1) * side] = re
            out[0, 1, here, b * side : (b + 1) * side] = im


def row_pass(plan, chunk, ins, blocks, result):
    side, tall = plan.length // RADIX, plan.rows // plan.strips
    specs, operands = [], []
    for part in range(plan.parts):
        at = 0 if part == plan.parts - 1 else chunk
        for array in ins[part]:
            specs.append(pl.BlockSpec((plan.per_part, 2, tall, LANES), lambda s, at=at: (0, 0, at, 0)))
            operands.append(array)
    specs.append(pl.BlockSpec((RADIX, 2, 2, side, side), lambda s: (0, 0, 0, 0, 0)))
    operands.append(blocks)
    aliases = {}
    if result is not None:
        specs.append(pl.BlockSpec(memory_space=pl.ANY))
        operands.append(result)
        aliases = {len(operands) - 1: 0}
    return pl.pallas_call(
        functools.partial(row_kernel, plan),
        grid=(1,),
        out_shape=jax.ShapeDtypeStruct((1, 2, plan.rows, plan.length), f32),
        in_specs=specs,
        out_specs=pl.BlockSpec((1, 2, tall, plan.length), lambda s, chunk=chunk: (0, 0, chunk, 0)),
        scratch_shapes=[
            pltpu.VMEM((plan.units, 2, tall, LANES), f32),
            pltpu.VMEM((RADIX, 2, tall, side), bf16),
            pltpu.VMEM((RADIX, 2, tall, side), bf16),
            pltpu.VMEM((RADIX, 2, tall, side), f32),
        ],
        input_output_aliases=aliases,
        compiler_params=pltpu.CompilerParams(vmem_limit_bytes=48 * MIB),
        cost_estimate=pl.CostEstimate(flops=6 * MIB * 1024 // plan.strips, bytes_accessed=20 * MIB // plan.strips, transcendentals=0),
        name=f"row_pass_{chunk}",
    )(*operands)


def jumped(array, axis, jump):
    return lax.ppermute(array, axis, [(i, i ^ jump) for i in range(lax.axis_size(axis))])


def moved(array, step):
    pairs = lax.axis_size("dist") // 2
    return lax.ppermute(
        array, "dist", [(2 * p + y, 2 * (p + step) + y) for p in range(pairs) if 0 <= p + step < pairs for y in range(2)]
    )


def pick(which, cases):
    return cases[0] if len(cases) == 1 else lax.select_n(which, *cases) if len(cases) > 2 else jnp.where(which == 0, *cases)


def along(piece):
    pairs = lax.axis_size("dist") // 2
    pair = lax.axis_index("dist") // 2
    up, down, mine = {0: piece}, {0: piece}, []
    for k in range(pairs):
        if k:
            up[k], down[k] = moved(up[k - 1], 1), moved(down[k - 1], -1)
        offsets = [(p ^ k) - p for p in range(pairs)]
        kinds = sorted(set(offsets))
        which = jnp.asarray([kinds.index(o) for o in offsets], jnp.int32)[pair] if len(kinds) > 1 else 0
        mine.append(pick(which, [down[o] if o >= 0 else up[-o] for o in kinds]))
    return mine


def spread(plan, mine):
    low, dists, group = plan.low, plan.dists, plan.group
    me = lax.axis_index("rows")
    if low == 2:
        to = lambda c, other: [
            ((d * group + 2 * h + c), ((d ^ 1 if other[0] else d) * group + 2 * h + other[1]))
            for d in range(dists)
            for h in range(plan.high)
        ]
        both = ("dist", "rows")
        found = []
        for piece in mine:
            own = lax.ppermute(piece, both, to(1, (1, 1)))
            other = lax.ppermute(piece, both, to(0, (1, 1)) + to(1, (0, 0)))
            found.append([[piece, own], [other]])
        return found
    pieces = [piece for pair in mine for piece in (pair, jumped(pair, "dist", 1))]
    found = []
    for g in range(plan.picks):
        cases = pieces[g * low : (g + 1) * low]
        blocks = [pick(jnp.bitwise_xor(me % low, l), cases) for l in range(low)]
        found.append([[jumped(block, "rows", l) if l else block] for l, block in enumerate(blocks)])
    return found


def body(wave, object_slice, fresnel):
    plan = Plan(wave)
    group, high, low = plan.group, plan.high, plan.low
    me = lax.axis_index("rows")

    width = object_slice.shape[2] // high
    held = []
    for j in range(high):
        to = jnp.bitwise_xor(me, j * low) // low
        block = lax.dynamic_slice_in_dim(object_slice, to * width, width, 2)
        held.append(jumped(block, "rows", j * low) if j else block)

    packed = pack(plan, wave)
    packed, held[0] = lax.optimization_barrier((packed, held[0]))
    sent = [[jumped(block, "rows", j) if j else block for j, block in enumerate(blocks)] for blocks in packed]

    blocks = circulant_blocks(fresnel, plan.length)
    slices = spread(plan, along(transmission(held)))

    arrived = []
    for part in range(plan.parts):
        outs = column_pass(plan, part, sent[part], slices[part * plan.per_part : (part + 1) * plan.per_part], blocks)
        back = [[None] * group for _ in outs[0]]
        for r in range(len(outs[0])):
            for j in plan.order:
                back[r][j] = jumped(outs[j][r], "rows", j) if j else outs[j][r]
        arrived.append(back)

    result = None
    for chunk in range(plan.strips):
        ins = [arrived[part][0] for part in range(plan.parts - 1)] + [arrived[-1][chunk]]
        result = row_pass(plan, chunk, ins, blocks, result)
    return result


def solution(mesh):
    return jax.shard_map(
        body,
        mesh=mesh,
        in_specs=(P("dist", None, "rows", None), P(None, "rows", "dist"), P("dist")),
        out_specs=P("dist", None, "rows", None),
        check_vma=False,
    )
```

```python
import functools
import math

import jax
import jax.numpy as jnp
import numpy as np
from jax import lax
from jax.experimental import pallas as pl
from jax.experimental.pallas import tpu as pltpu
from jax.sharding import PartitionSpec as P

f32, bf16 = jnp.float32, jnp.bfloat16
LANES = 128
RADIX = 8
STRIP = 32
ROW_STRIP = 16
GROUPS = 4
SPARE = 8
MIB = 1 << 20
VMEM = 62 * MIB
ROOT = math.sqrt(0.5)


def turn(z, quarter):
    re, im = z
    return ((re, im), (-im, re), (-re, -im), (im, -re))[quarter % 4]


def plus(a, b):
    return (a[0] + b[0], a[1] + b[1])


def minus(a, b):
    return (a[0] - b[0], a[1] - b[1])


def dft4(z, sign):
    even, odd = plus(z[0], z[2]), plus(z[1], z[3])
    low, high = minus(z[0], z[2]), turn(minus(z[1], z[3]), sign)
    return [plus(even, odd), plus(low, high), minus(even, odd), minus(low, high)]


def dft8(z, sign):
    even, odd = dft4(z[0::2], sign), dft4(z[1::2], sign)
    (re1, im1), (re3, im3) = odd[1], odd[3]
    odd[1] = (ROOT * (re1 - sign * im1), ROOT * (im1 + sign * re1))
    odd[2] = turn(odd[2], sign)
    odd[3] = (-ROOT * (re3 + sign * im3), ROOT * (sign * re3 - im3))
    return [plus(a, b) for a, b in zip(even, odd)] + [minus(a, b) for a, b in zip(even, odd)]


def split(value):
    high = value.astype(bf16)
    return high, (value - high.astype(f32)).astype(bf16)


def dot3(a_high, a_low, b_high, b_low):
    dot = functools.partial(jnp.dot, preferred_element_type=f32)
    return dot(a_high, b_high) + (dot(a_high, b_low) + dot(a_low, b_high))


def blocks_kernel(response, wheel, right, twist, blocks):
    half = wheel.shape[1]
    k = pl.program_id(0)
    h_re, h_im = response[0, pl.ds(k, 1)], response[1, pl.ds(k, 1)]
    w_re, w_im = wheel[0], wheel[1]
    left = jnp.concatenate((w_re * h_re - w_im * h_im, w_re * h_im + w_im * h_re), axis=1)
    both = jnp.dot(left, right[...], precision=lax.Precision.HIGHEST, preferred_element_type=f32)
    both_re, both_im = both[:, :half], both[:, half:]
    t_re, t_im = twist[0, 0], twist[0, 1]
    high, low = split(both_re * t_re - both_im * t_im)
    blocks[0, 0, 0], blocks[0, 0, 1] = high, low
    high, low = split(both_re * t_im + both_im * t_re)
    blocks[0, 1, 0], blocks[0, 1, 1] = high, low


def circulant_blocks(fresnel, length):
    side = length // RADIX
    index = np.arange(RADIX)[:, None] + RADIX * np.arange(side)[None]
    freq = np.where(index < length // 2, index, index - length).astype(np.float32) / length
    phase = (-math.pi * fresnel[0]) * (freq * freq)
    response = jnp.stack((jnp.cos(phase), jnp.sin(phase)))
    line = np.arange(side)
    angle = 2 * np.pi / side * (line[:, None] * line[None] % side)
    wheel = np.stack((np.cos(angle), np.sin(angle))).astype(np.float32)
    scale = 1.0 / (side * RADIX)
    w_re, w_im = np.cos(angle).T * scale, np.sin(angle).T * scale
    right = np.block([[w_re, -w_im], [w_im, w_re]]).astype(np.float32)
    apart = np.arange(RADIX)[:, None, None] * (line[:, None] - line[None])
    twist = np.stack((np.cos(2 * np.pi / length * apart), np.sin(2 * np.pi / length * apart)), 1).astype(np.float32)
    whole = lambda *shape: pl.BlockSpec(shape, lambda k: (0,) * len(shape))
    return pl.pallas_call(
        blocks_kernel,
        grid=(RADIX,),
        out_shape=jax.ShapeDtypeStruct((RADIX, 2, 2, side, side), bf16),
        in_specs=[
            whole(2, RADIX, side),
            whole(2, side, side),
            whole(2 * side, 2 * side),
            pl.BlockSpec((1, 2, side, side), lambda k: (k, 0, 0, 0)),
        ],
        out_specs=pl.BlockSpec((1, 2, 2, side, side), lambda k: (k, 0, 0, 0, 0)),
        compiler_params=pltpu.CompilerParams(vmem_limit_bytes=VMEM),
        name="circulant_blocks",
    )(response, jnp.asarray(wheel), jnp.asarray(right), jnp.asarray(twist))


class Plan:
    def __init__(self, wave):
        self.group, self.dists = lax.axis_size("rows"), lax.axis_size("dist")
        self.rows, self.length = wave.shape[2], wave.shape[3]
        self.units = self.length // LANES
        self.high = min(self.units // self.dists, self.group)
        self.low = self.group // self.high
        self.picks = self.dists // self.low
        halves = self.picks == 4
        self.batches = [[0, 1], [2, 3]] if halves else [list(range(self.picks))]
        self.parts = [[0, 1], [2], [3]] if halves else [list(range(self.picks))]
        self.chunks = [self.rows // 2] * 2 if halves and self.rows // 4 >= LANES else [self.rows]
        self.sends = [([self.rows], True), ([self.rows], True), (self.chunks, False)] if halves else [([self.rows], True)]
        self.order = sorted(range(self.group), key=lambda jump: (-(jump // self.low), jump % self.low))

    def guest(self):
        return jnp.bitwise_xor(lax.axis_index("rows") % self.low, lax.axis_index("dist") % self.low)

    def unit(self, place, dist, pick):
        other = lax.rem(dist // self.low + (self.picks - pick), self.picks) * self.low + place % self.low
        return other * self.high + place // self.low


def outputs(plan, chunks, merged, near, far):
    nears = [near(plan.rows) for _ in range(plan.low)]
    if merged:
        return nears + [far(plan.rows) for _ in range(plan.high - 1)]
    return nears + [near(rows) for _ in range(plan.low, plan.group) for rows in chunks]


def shapes(plan, picks, chunks, merged, spare=0):
    shape = lambda *dims: jax.ShapeDtypeStruct(dims, f32)
    return outputs(
        plan,
        chunks,
        merged,
        lambda rows: shape(picks, 2, rows, LANES),
        lambda rows: shape(plan.low, picks, 2, rows + spare, LANES),
    )


def target(plan, outs, jump):
    high, low = jump // plan.low, jump % plan.low
    return outs[plan.low + high - 1].at[low] if high else outs[low]


def pack_kernel(plan, wave, *refs):
    outs, (staged, ins, sems) = refs[:-3], refs[-3:]
    me, dist = lax.axis_index("rows"), lax.axis_index("dist")
    size = len(outs) // len(plan.batches)
    loads, stores = [], []
    for batch, picks in enumerate(plan.batches):
        for jump in plan.order:
            for at, pick in enumerate(picks):
                slot = len(loads)
                unit = plan.unit(jnp.bitwise_xor(me, jump), dist, pick)
                start = pl.multiple_of(unit * LANES, LANES)
                out = target(plan, outs[batch * size : (batch + 1) * size], jump).at[at, :, pl.ds(0, plan.rows)]
                loads.append(pltpu.make_async_copy(wave.at[0, :, :, pl.ds(start, LANES)], staged.at[slot], ins.at[slot]))
                stores.append(pltpu.make_async_copy(staged.at[slot], out, sems.at[slot]))
    for load in loads:
        load.start()
    for load, store in zip(loads, stores):
        load.wait()
        store.start()
    for store in stores:
        store.wait()


def pack(plan, wave):
    outs = [shape for picks in plan.batches for shape in shapes(plan, len(picks), [plan.rows], True, SPARE)]
    hbm = pl.BlockSpec(memory_space=pltpu.HBM)
    outs = pl.pallas_call(
        functools.partial(pack_kernel, plan),
        out_shape=outs,
        in_specs=[hbm],
        out_specs=[hbm] * len(outs),
        scratch_shapes=[
            pltpu.VMEM((plan.units, 2, plan.rows, LANES), f32),
            pltpu.SemaphoreType.DMA((plan.units,)),
            pltpu.SemaphoreType.DMA((plan.units,)),
        ],
        compiler_params=pltpu.CompilerParams(vmem_limit_bytes=VMEM),
        cost_estimate=pl.CostEstimate(flops=0, bytes_accessed=16 * MIB, transcendentals=0),
        name="pack",
    )(wave)
    size = len(outs) // len(plan.batches)
    return [outs[batch * size : (batch + 1) * size] for batch in range(len(plan.batches))]


def series(square, first, count):
    total = jnp.ones_like(square)
    for i in reversed(range(count)):
        total = 1.0 - square * (1.0 / ((first + 2 * i) * (first + 2 * i + 1))) * total
    return total


def transmission_kernel(*refs):
    out = refs[-1]
    for h, piece in enumerate(refs[:-1]):
        amplitude, square = jnp.exp(-piece[1]), piece[0] * piece[0]
        out[h, 0] = amplitude * series(square, 1, 7)
        out[h, 1] = amplitude * (piece[0] * series(square, 2, 7))


def transmission(held):
    rows = held[0].shape[1]
    tall = min(rows, LANES)
    return pl.pallas_call(
        transmission_kernel,
        grid=(rows // tall,),
        out_shape=jax.ShapeDtypeStruct((len(held),) + held[0].shape, f32),
        in_specs=[pl.BlockSpec((2, tall, LANES), lambda s: (0, s, 0))] * len(held),
        out_specs=pl.BlockSpec((len(held), 2, tall, LANES), lambda s: (0, 0, s, 0)),
        compiler_params=pltpu.CompilerParams(vmem_limit_bytes=VMEM),
        name="transmission",
    )(*held)


def column_kernel(plan, counts, merged, *refs):
    n = plan.group
    waves, refs = [refs[g * n : (g + 1) * n] for g in range(len(counts))], refs[len(counts) * n :]
    slices = []
    for count in counts:
        slices.append(refs[:count])
        refs = refs[count:]
    blocks, outs = refs[0], refs[1:-4]
    field, x_high, x_low, y = refs[-4:]
    me, step = lax.axis_index("rows"), pl.program_id(0)
    rows, side = plan.rows, plan.length // RADIX
    for g in range(len(counts)):
        for jump in range(n):

            @pl.when(step == g)
            def _(g=g, jump=jump, cases=slices[g]):
                base = jnp.bitwise_xor(me, jump) * rows

                @pl.loop(0, rows // STRIP)
                def _(s):
                    here = pl.ds(pl.multiple_of(s * STRIP, STRIP), STRIP)
                    read = lambda c: pick(plan.guest(), [case[jump, c, here] for case in cases])
                    t_re, t_im = read(0), read(1)
                    w_re, w_im = waves[g][jump][0, here], waves[g][jump][1, here]
                    there = pl.ds(pl.multiple_of(base + s * STRIP, STRIP), STRIP)
                    field[0, there] = w_re * t_re - w_im * t_im
                    field[1, there] = w_re * t_im + w_im * t_re

    @pl.loop(0, side // STRIP)
    def _(s):
        at = lambda b: pl.ds(pl.multiple_of(b * side + s * STRIP, STRIP), STRIP)
        here = pl.ds(pl.multiple_of(s * STRIP, STRIP), STRIP)
        for k, z in enumerate(dft8([(field[0, at(b)], field[1, at(b)]) for b in range(RADIX)], -1)):
            x_high[k, here], x_low[k, here] = split(jnp.concatenate(z, axis=1))

    @pl.loop(0, RADIX)
    def _(k):
        by_re = dot3(blocks[k, 0, 0], blocks[k, 0, 1], x_high[k], x_low[k])
        by_im = dot3(blocks[k, 1, 0], blocks[k, 1, 1], x_high[k], x_low[k])
        y[k, :, :LANES] = by_re[:, :LANES] - by_im[:, LANES:]
        y[k, :, LANES:] = by_re[:, LANES:] + by_im[:, :LANES]

    @pl.loop(0, side // STRIP)
    def _(s):
        here = pl.ds(pl.multiple_of(s * STRIP, STRIP), STRIP)
        for b, z in enumerate(dft8([(y[k, here, :LANES], y[k, here, LANES:]) for k in range(RADIX)], 1)):
            there = pl.ds(pl.multiple_of(b * side + s * STRIP, STRIP), STRIP)
            field[0, there], field[1, there] = z

    for jump in range(n):
        start = jnp.bitwise_xor(me, jump) * rows
        if jump < plan.low or merged:
            there = pl.ds(pl.multiple_of(start, rows), rows)
            out = target(plan, outs, jump)
            out[0, 0], out[0, 1] = field[0, there], field[1, there]
            continue
        count = (len(outs) - plan.low) // (n - plan.low)
        for out in outs[plan.low + (jump - plan.low) * count :][:count]:
            tall = out.shape[2]
            there = pl.ds(pl.multiple_of(start, tall), tall)
            out[0, 0], out[0, 1] = field[0, there], field[1, there]
            start += tall


def taken(array, rows, start, picks, pick):
    lead = (pl.squeezed,) * (array.ndim - 4)
    return pl.BlockSpec(lead + (picks, 2, rows, LANES), lambda g: (0,) * len(lead) + (pick(g), 0, start, 0))


def column_pass(plan, part, waves, slices, blocks):
    side = plan.length // RADIX
    picks = len(plan.parts[part])
    chunks, merged = plan.sends[part]
    flat = [array for cases in slices for array in cases]
    slice_spec = pl.BlockSpec((plan.group, 2, plan.rows, LANES), lambda g: (0, 0, 0, 0))
    return pl.pallas_call(
        functools.partial(column_kernel, plan, [len(cases) for cases in slices], merged),
        grid=(picks,),
        out_shape=shapes(plan, picks, chunks, merged, SPARE),
        in_specs=[taken(array, plan.rows, 0, pl.squeezed, lambda g, at=at: at) for of in waves for array, at in of]
        + [slice_spec] * len(flat)
        + [pl.BlockSpec((RADIX, 2, 2, side, side), lambda g: (0, 0, 0, 0, 0))],
        out_specs=outputs(
            plan,
            chunks,
            merged,
            lambda rows: pl.BlockSpec((1, 2, rows, LANES), lambda g: (g, 0, 0, 0)),
            lambda rows: pl.BlockSpec((plan.low, 1, 2, rows, LANES), lambda g: (0, g, 0, 0, 0)),
        ),
        scratch_shapes=[
            pltpu.VMEM((2, plan.length, LANES), f32),
            pltpu.VMEM((RADIX, side, 2 * LANES), bf16),
            pltpu.VMEM((RADIX, side, 2 * LANES), bf16),
            pltpu.VMEM((RADIX, side, 2 * LANES), f32),
        ],
        compiler_params=pltpu.CompilerParams(vmem_limit_bytes=VMEM),
        cost_estimate=pl.CostEstimate(flops=0, bytes_accessed=1024, transcendentals=0),
        name=f"column_pass_{part}",
    )(*[array for of in waves for array, _ in of], *flat, blocks)


def row_kernel(plan, chunk, *refs):
    n = plan.group
    ins, blocks, out = refs[: len(plan.parts) * n], refs[len(plan.parts) * n], refs[-9]
    field, d, x, y, staged, in_sems, d_sem, out_sems = refs[-8:]
    me, dist = lax.axis_index("rows"), lax.axis_index("dist")
    side, tall = plan.length // RADIX, plan.chunks[chunk]
    first = sum(plan.chunks[:chunk])
    group = tall // GROUPS
    loads = [[] for _ in range(GROUPS)]
    for r in range(GROUPS):
        here = pl.ds(r * group, group)
        for part, picks in enumerate(plan.parts):
            for jump in range(n):
                array = ins[part * n + jump]
                start = r * group + (0 if array.shape[-2] == tall else first)
                array = array.at[0] if len(array.shape) > 4 else array
                for g, pick in enumerate(picks):
                    unit = plan.unit(jnp.bitwise_xor(me, jump), dist, pick)
                    sem = in_sems.at[r, len(loads[r])]
                    loads[r].append(pltpu.make_async_copy(array.at[g, :, pl.ds(start, group)], field.at[unit, :, here], sem))
    load_blocks = pltpu.make_async_copy(blocks, d, d_sem)
    for load in loads[0]:
        load.start()
    load_blocks.start()
    for of in loads[1:]:
        for load in of:
            load.start()
    wide = side // LANES

    for r in range(GROUPS):
        for load in loads[r]:
            load.wait()

        @pl.loop(0, group // ROW_STRIP)
        def _(s, r=r):
            here = pl.ds(pl.multiple_of(r * group + s * ROW_STRIP, ROW_STRIP), ROW_STRIP)
            line = lambda b, c: jnp.concatenate([field[b * wide + v, c, here] for v in range(wide)], axis=1)
            for k, z in enumerate(dft8([(line(b, 0), line(b, 1)) for b in range(RADIX)], -1)):
                for c in range(2):
                    x[k, 0, c, here], x[k, 1, c, here] = split(z[c])

    load_blocks.wait()

    @pl.loop(0, RADIX)
    def _(k):
        back = lax.rem(RADIX - k, RADIX)
        both = x[k].reshape(4 * tall, side)
        high = both[: 2 * tall]

        def by(c):
            product = jnp.dot(both, d[back, c, 0], preferred_element_type=f32)
            return product[: 2 * tall] + product[2 * tall :] + jnp.dot(high, d[back, c, 1], preferred_element_type=f32)

        by_re, by_im = by(0), by(1)
        y[k, 0] = by_re[:tall] - by_im[tall:]
        y[k, 1] = by_re[tall:] + by_im[:tall]

    stores = []
    for r in range(GROUPS):

        @pl.loop(0, group // ROW_STRIP)
        def _(s, r=r):
            here = pl.ds(pl.multiple_of(r * group + s * ROW_STRIP, ROW_STRIP), ROW_STRIP)
            for b, z in enumerate(dft8([(y[k, 0, here], y[k, 1, here]) for k in range(RADIX)], 1)):
                staged[0, here, b * side : (b + 1) * side], staged[1, here, b * side : (b + 1) * side] = z

        stores.append(
            pltpu.make_async_copy(
                staged.at[:, pl.ds(r * group, group)], out.at[0, :, pl.ds(first + r * group, group)], out_sems.at[r]
            )
        )
        stores[-1].start()
    for store in stores:
        store.wait()


def row_pass(plan, chunk, ins, blocks, result):
    side, tall = plan.length // RADIX, plan.chunks[chunk]
    operands = [array for of in ins for array in of] + [blocks]
    aliases = {}
    if result is not None:
        operands.append(result)
        aliases = {len(operands) - 1: 0}
    return pl.pallas_call(
        functools.partial(row_kernel, plan, chunk),
        out_shape=jax.ShapeDtypeStruct((1, 2, plan.rows, plan.length), f32),
        in_specs=[pl.BlockSpec(memory_space=pl.ANY)] * len(operands),
        out_specs=pl.BlockSpec(memory_space=pltpu.HBM),
        scratch_shapes=[
            pltpu.VMEM((plan.units, 2, tall, LANES), f32),
            pltpu.VMEM((RADIX, 2, 2, side, side), bf16),
            pltpu.VMEM((RADIX, 2, 2, tall, side), bf16),
            pltpu.VMEM((RADIX, 2, tall, side), f32),
            pltpu.VMEM((2, tall, plan.length), f32),
            pltpu.SemaphoreType.DMA((GROUPS, plan.units)),
            pltpu.SemaphoreType.DMA,
            pltpu.SemaphoreType.DMA((GROUPS,)),
        ],
        input_output_aliases=aliases,
        compiler_params=pltpu.CompilerParams(vmem_limit_bytes=VMEM),
        cost_estimate=pl.CostEstimate(flops=6 * MIB * 1024 * tall // plan.rows, bytes_accessed=20 * MIB * tall // plan.rows, transcendentals=0),
        name=f"row_pass_{chunk}",
    )(*operands)


def jumped(array, axis, jump):
    return lax.ppermute(array, axis, [(i, i ^ jump) for i in range(lax.axis_size(axis))])


def pick(which, cases):
    return cases[0] if len(cases) == 1 else lax.select_n(which, *cases) if len(cases) > 2 else jnp.where(which == 0, *cases)


def after(array, *others):
    return lax.optimization_barrier((array, *others))[0]


def piece_of(object_slice, place, plan):
    width = object_slice.shape[2] // plan.high
    return lax.dynamic_slice_in_dim(object_slice, place // plan.low * width, width, 2)


def owned(plan, object_slice):
    me = lax.axis_index("rows")
    blocks = [piece_of(object_slice, jnp.bitwise_xor(me, h * 2), plan) for h in range(plan.high)]
    held = [blocks[0]]
    for jump in range(1, plan.group):
        pairs = [
            (d * plan.group + (i ^ jump), d * plan.group + i)
            for d in range(plan.dists)
            for i in range(plan.group)
            if i % 2 == d % 2
        ]
        held.append(lax.ppermute(blocks[jump // 2], ("dist", "rows"), pairs))
    return held


def owners_round(plan, through, blocks, first):
    group, dists = plan.group, plan.dists
    lines = lambda to: [(d * group + i, to(d) * group + i) for d in range(dists) for i in range(group) if i % 2 == d % 2]
    both = ("dist", "rows")
    mine, last = [through], []
    for g in range(1, plan.picks):
        mine.append(lax.ppermute(mine[-1], both, lines(lambda d: (d + 2) % dists)))
    for g in range(plan.picks):
        held = after(mine[g], blocks, first, *last) if g else through
        last = [lax.ppermute(held, both, lines(lambda d: d ^ 1))]
        wait = yield [held, last[0]]
        last += wait or []


def spread(plan, through):
    me, dist = lax.axis_index("rows"), lax.axis_index("dist")
    pieces = lax.all_gather(through, "dist")
    found = []
    for g in range(plan.picks):
        first = lax.rem(dist // plan.low + (plan.picks - g), plan.picks) * plan.low
        parts = []
        for l in range(plan.low):
            block = lax.dynamic_index_in_dim(pieces, first + jnp.bitwise_xor(me % plan.low, l), keepdims=False)
            parts.append(jumped(block, "rows", l) if l else block)
        found.append([jnp.stack(parts, 1).reshape((plan.group,) + through.shape[1:])])
    return found


def sent_far(plan, outs, ahead=()):
    return [jumped(after(block, *ahead), "rows", h * plan.low) for h, block in enumerate(outs[plan.low :], 1)]


def sent_near(plan, outs):
    return [jumped(block, "rows", l) if l else block for l, block in enumerate(outs[: plan.low])]


def sent_on(plan, far, ahead=()):
    got = []
    for block in far:
        got.append(block)
        onward = after(block, *ahead)
        got += [jumped(onward[l], "rows", l) for l in range(1, plan.low)]
    return got


def body(wave, object_slice, fresnel):
    plan = Plan(wave)
    group, high, low = plan.group, plan.high, plan.low
    me = lax.axis_index("rows")

    if low == 2:
        held = owned(plan, object_slice)
    else:
        held = [piece_of(object_slice, jnp.bitwise_xor(me, h * low), plan) for h in range(high)]
        held = [jumped(block, "rows", h * low) if h else block for h, block in enumerate(held)]

    packed = pack(plan, wave)
    held[0] = after(held[0], *[block for blocks in packed for block in blocks])
    sent = [sent_near(plan, outs) + sent_on(plan, sent_far(plan, outs)) for outs in packed]
    waves = [[(array, at) for array in got] for got, picks in zip(sent, plan.batches) for at in range(len(picks))]

    through = transmission(held)
    blocks = circulant_blocks(after(fresnel, through), plan.length)
    rounds = owners_round(plan, through, blocks, sent[0][low]) if low == 2 else iter(spread(plan, through))

    gone, flown, slices, last = [], [], [], len(plan.parts) - 1
    for part, picks in enumerate(plan.parts):
        while len(slices) <= picks[-1]:
            wait = [sent[-1][low], outs[0]] if low == 2 and len(slices) == 2 else None
            slices.append(rounds.send(wait) if wait else next(rounds))
        here = slice(picks[0], picks[-1] + 1)
        if part and part == last:
            gone[0] += sent_on(plan, flown[0], outs[:1])
            blocks = after(blocks, *[block for of in gone for block in of if not any(block is each for each in flown[1])])
        outs = column_pass(plan, part, waves[here], slices[here], blocks)
        gone.append(sent_near(plan, outs))
        if plan.sends[part][1]:
            flown.append(sent_far(plan, outs, [sent[-1][j] for j in range(low, group, low)] if last else []))
    result, count = None, len(plan.chunks)
    if not last:
        gone[0] += sent_on(plan, flown[0])
    for chunk in range(count):
        ins = list(gone)
        if last:
            far = [outs[low + (j - low) * count + chunk] for j in range(low, group)]
            far = [jumped(block, "rows", j) for j, block in enumerate(far, low)]
            if chunk == 0:
                gone[1] += sent_on(plan, flown[1], far[:1])
            ins[-1] = gone[-1] + far
        result = row_pass(plan, chunk, ins, blocks, result)
    return result


def solution(mesh):
    return jax.shard_map(
        body,
        mesh=mesh,
        in_specs=(P("dist", None, "rows", None), P(None, "rows", "dist"), P("dist")),
        out_specs=P("dist", None, "rows", None),
        check_vma=False,
    )
```

```python
import functools
import math

import jax
import jax.numpy as jnp
import numpy as np
from jax import lax
from jax.experimental import pallas as pl
from jax.experimental.pallas import tpu as pltpu
from jax.sharding import PartitionSpec as P

f32, bf16 = jnp.float32, jnp.bfloat16
LANES = 128
RADIX = 8
STRIP = 32
ROW_STRIP = 16
GROUPS = 4
SPARE = 8
MIB = 1 << 20
VMEM = 64 * MIB - 256 * 1024
EARLY_VMEM = 56 * MIB
ROOT = math.sqrt(0.5)


def turn(z, quarter):
    re, im = z
    return ((re, im), (-im, re), (-re, -im), (im, -re))[quarter % 4]


def plus(a, b):
    return (a[0] + b[0], a[1] + b[1])


def minus(a, b):
    return (a[0] - b[0], a[1] - b[1])


def dft4(z, sign):
    even, odd = plus(z[0], z[2]), plus(z[1], z[3])
    low, high = minus(z[0], z[2]), turn(minus(z[1], z[3]), sign)
    return [plus(even, odd), plus(low, high), minus(even, odd), minus(low, high)]


def dft8(z, sign):
    even, odd = dft4(z[0::2], sign), dft4(z[1::2], sign)
    (re1, im1), (re3, im3) = odd[1], odd[3]
    odd[1] = (ROOT * (re1 - sign * im1), ROOT * (im1 + sign * re1))
    odd[2] = turn(odd[2], sign)
    odd[3] = (-ROOT * (re3 + sign * im3), ROOT * (sign * re3 - im3))
    return [plus(a, b) for a, b in zip(even, odd)] + [minus(a, b) for a, b in zip(even, odd)]


def split(value):
    high = value.astype(bf16)
    return high, (value - high.astype(f32)).astype(bf16)


def dot3(a_high, a_low, b_high, b_low):
    dot = functools.partial(jnp.dot, preferred_element_type=f32)
    return dot(a_high, b_high) + (dot(a_high, b_low) + dot(a_low, b_high))


def blocks_kernel(response, wheel, right, twist, blocks):
    half = wheel.shape[1]
    k = pl.program_id(0)
    h_re, h_im = response[0, pl.ds(k, 1)], response[1, pl.ds(k, 1)]
    w_re, w_im = wheel[0], wheel[1]
    left = jnp.concatenate((w_re * h_re - w_im * h_im, w_re * h_im + w_im * h_re), axis=1)
    both = jnp.dot(left, right[...], precision=lax.Precision.HIGHEST, preferred_element_type=f32)
    both_re, both_im = both[:, :half], both[:, half:]
    t_re, t_im = twist[0, 0], twist[0, 1]
    high, low = split(both_re * t_re - both_im * t_im)
    blocks[0, 0, 0], blocks[0, 0, 1] = high, low
    high, low = split(both_re * t_im + both_im * t_re)
    blocks[0, 1, 0], blocks[0, 1, 1] = high, low


def circulant_blocks(fresnel, length):
    side = length // RADIX
    index = np.arange(RADIX)[:, None] + RADIX * np.arange(side)[None]
    freq = np.where(index < length // 2, index, index - length).astype(np.float32) / length
    phase = (-math.pi * fresnel[0]) * (freq * freq)
    response = jnp.stack((jnp.cos(phase), jnp.sin(phase)))
    line = np.arange(side)
    angle = 2 * np.pi / side * (line[:, None] * line[None] % side)
    wheel = np.stack((np.cos(angle), np.sin(angle))).astype(np.float32)
    scale = 1.0 / (side * RADIX)
    w_re, w_im = np.cos(angle).T * scale, np.sin(angle).T * scale
    right = np.block([[w_re, -w_im], [w_im, w_re]]).astype(np.float32)
    apart = np.arange(RADIX)[:, None, None] * (line[:, None] - line[None])
    twist = np.stack((np.cos(2 * np.pi / length * apart), np.sin(2 * np.pi / length * apart)), 1).astype(np.float32)
    whole = lambda *shape: pl.BlockSpec(shape, lambda k: (0,) * len(shape))
    return pl.pallas_call(
        blocks_kernel,
        grid=(RADIX,),
        out_shape=jax.ShapeDtypeStruct((RADIX, 2, 2, side, side), bf16),
        in_specs=[
            whole(2, RADIX, side),
            whole(2, side, side),
            whole(2 * side, 2 * side),
            pl.BlockSpec((1, 2, side, side), lambda k: (k, 0, 0, 0)),
        ],
        out_specs=pl.BlockSpec((1, 2, 2, side, side), lambda k: (k, 0, 0, 0, 0)),
        compiler_params=pltpu.CompilerParams(vmem_limit_bytes=EARLY_VMEM),
        name="circulant_blocks",
    )(response, jnp.asarray(wheel), jnp.asarray(right), jnp.asarray(twist))


class Plan:
    def __init__(self, wave):
        self.group, self.dists = lax.axis_size("rows"), lax.axis_size("dist")
        self.rows, self.length = wave.shape[2], wave.shape[3]
        self.units = self.length // LANES
        self.high = min(self.units // self.dists, self.group)
        self.low = self.group // self.high
        self.picks = self.dists // self.low
        halves = self.picks == 4
        self.batches = [[0, 1], [2, 3]] if halves else [list(range(self.picks))]
        self.parts = [[0, 1], [2], [3]] if halves else [list(range(self.picks))]
        self.chunks = [self.rows // 2] * 2 if halves and self.rows // 4 >= LANES else [self.rows]
        self.sends = [([self.rows], True), ([self.rows], False), (self.chunks, False)] if halves else [([self.rows], True)]
        self.order = sorted(range(self.group), key=lambda jump: (-(jump // self.low), jump % self.low))

    def guest(self):
        return jnp.bitwise_xor(lax.axis_index("rows") % self.low, lax.axis_index("dist") % self.low)

    def unit(self, place, dist, pick):
        other = lax.rem(dist // self.low + (self.picks - pick), self.picks) * self.low + place % self.low
        return other * self.high + place // self.low


def outputs(plan, chunks, merged, near, far, direct):
    nears = [near(plan.rows) for _ in range(plan.low)]
    if merged:
        return nears + [far(plan.rows) for _ in range(plan.high - 1)]
    return nears + [direct(rows) for _ in range(plan.low, plan.group) for rows in chunks]


def shapes(plan, picks, chunks, merged, spare=0):
    shape = lambda *dims: jax.ShapeDtypeStruct(dims, f32)
    return outputs(
        plan,
        chunks,
        merged,
        lambda rows: shape(picks, 2, rows, LANES),
        lambda rows: shape(plan.low, picks, 2, rows + spare, LANES),
        lambda rows: shape(picks, 2, rows + (spare if rows == plan.rows else 0), LANES),
    )


def target(plan, outs, jump):
    high, low = jump // plan.low, jump % plan.low
    return outs[plan.low + high - 1].at[low] if high else outs[low]


def pack_kernel(plan, wave, *refs):
    outs, (staged, ins, sems) = refs[:-3], refs[-3:]
    me, dist = lax.axis_index("rows"), lax.axis_index("dist")
    size = len(outs) // len(plan.batches)
    loads, stores = [], []
    for batch, picks in enumerate(plan.batches):
        for jump in plan.order:
            for at, pick in enumerate(picks):
                slot = len(loads)
                unit = plan.unit(jnp.bitwise_xor(me, jump), dist, pick)
                start = pl.multiple_of(unit * LANES, LANES)
                out = target(plan, outs[batch * size : (batch + 1) * size], jump).at[at, :, pl.ds(0, plan.rows)]
                loads.append(pltpu.make_async_copy(wave.at[0, :, :, pl.ds(start, LANES)], staged.at[slot], ins.at[slot]))
                stores.append(pltpu.make_async_copy(staged.at[slot], out, sems.at[slot]))
    for load in loads:
        load.start()
    for load, store in zip(loads, stores):
        load.wait()
        store.start()
    for store in stores:
        store.wait()


def pack(plan, wave):
    outs = [shape for picks in plan.batches for shape in shapes(plan, len(picks), [plan.rows], True, SPARE)]
    hbm = pl.BlockSpec(memory_space=pltpu.HBM)
    outs = pl.pallas_call(
        functools.partial(pack_kernel, plan),
        out_shape=outs,
        in_specs=[hbm],
        out_specs=[hbm] * len(outs),
        scratch_shapes=[
            pltpu.VMEM((plan.units, 2, plan.rows, LANES), f32),
            pltpu.SemaphoreType.DMA((plan.units,)),
            pltpu.SemaphoreType.DMA((plan.units,)),
        ],
        compiler_params=pltpu.CompilerParams(vmem_limit_bytes=EARLY_VMEM),
        cost_estimate=pl.CostEstimate(flops=0, bytes_accessed=16 * MIB, transcendentals=0),
        name="pack",
    )(wave)
    size = len(outs) // len(plan.batches)
    return [outs[batch * size : (batch + 1) * size] for batch in range(len(plan.batches))]


def series(square, first, count):
    total = jnp.ones_like(square)
    for i in reversed(range(count)):
        total = 1.0 - square * (1.0 / ((first + 2 * i) * (first + 2 * i + 1))) * total
    return total


def transmission_kernel(*refs):
    out = refs[-1]
    for h, piece in enumerate(refs[:-1]):
        amplitude, square = jnp.exp(-piece[1]), piece[0] * piece[0]
        out[h, 0] = amplitude * series(square, 1, 7)
        out[h, 1] = amplitude * (piece[0] * series(square, 2, 7))


def transmission(held):
    rows = held[0].shape[1]
    tall = min(rows, LANES)
    return pl.pallas_call(
        transmission_kernel,
        grid=(rows // tall,),
        out_shape=jax.ShapeDtypeStruct((len(held),) + held[0].shape, f32),
        in_specs=[pl.BlockSpec((2, tall, LANES), lambda s: (0, s, 0))] * len(held),
        out_specs=pl.BlockSpec((len(held), 2, tall, LANES), lambda s: (0, 0, s, 0)),
        compiler_params=pltpu.CompilerParams(vmem_limit_bytes=EARLY_VMEM),
        name="transmission",
    )(*held)


def column_kernel(plan, counts, merged, *refs):
    n = plan.group
    waves, refs = [refs[g * n : (g + 1) * n] for g in range(len(counts))], refs[len(counts) * n :]
    slices = []
    for count in counts:
        slices.append(refs[:count])
        refs = refs[count:]
    blocks, outs = refs[0], refs[1:-4]
    field, x_high, x_low, y = refs[-4:]
    me, step = lax.axis_index("rows"), pl.program_id(0)
    rows, side = plan.rows, plan.length // RADIX
    for g in range(len(counts)):
        for jump in range(n):

            @pl.when(step == g)
            def _(g=g, jump=jump, cases=slices[g]):
                base = jnp.bitwise_xor(me, jump) * rows

                @pl.loop(0, rows // STRIP)
                def _(s):
                    here = pl.ds(pl.multiple_of(s * STRIP, STRIP), STRIP)
                    read = lambda c: pick(plan.guest(), [case[jump, c, here] for case in cases])
                    t_re, t_im = read(0), read(1)
                    w_re, w_im = waves[g][jump][0, here], waves[g][jump][1, here]
                    there = pl.ds(pl.multiple_of(base + s * STRIP, STRIP), STRIP)
                    field[0, there] = w_re * t_re - w_im * t_im
                    field[1, there] = w_re * t_im + w_im * t_re

    @pl.loop(0, side // STRIP)
    def _(s):
        at = lambda b: pl.ds(pl.multiple_of(b * side + s * STRIP, STRIP), STRIP)
        here = pl.ds(pl.multiple_of(s * STRIP, STRIP), STRIP)
        for k, z in enumerate(dft8([(field[0, at(b)], field[1, at(b)]) for b in range(RADIX)], -1)):
            x_high[k, here], x_low[k, here] = split(jnp.concatenate(z, axis=1))

    @pl.loop(0, RADIX)
    def _(k):
        by_re = dot3(blocks[k, 0, 0], blocks[k, 0, 1], x_high[k], x_low[k])
        by_im = dot3(blocks[k, 1, 0], blocks[k, 1, 1], x_high[k], x_low[k])
        y[k, :, :LANES] = by_re[:, :LANES] - by_im[:, LANES:]
        y[k, :, LANES:] = by_re[:, LANES:] + by_im[:, :LANES]

    @pl.loop(0, side // STRIP)
    def _(s):
        here = pl.ds(pl.multiple_of(s * STRIP, STRIP), STRIP)
        for b, z in enumerate(dft8([(y[k, here, :LANES], y[k, here, LANES:]) for k in range(RADIX)], 1)):
            there = pl.ds(pl.multiple_of(b * side + s * STRIP, STRIP), STRIP)
            field[0, there], field[1, there] = z

    for jump in range(n):
        start = jnp.bitwise_xor(me, jump) * rows
        if jump < plan.low or merged:
            there = pl.ds(pl.multiple_of(start, rows), rows)
            out = target(plan, outs, jump)
            out[0, 0], out[0, 1] = field[0, there], field[1, there]
            continue
        count = (len(outs) - plan.low) // (n - plan.low)
        for out in outs[plan.low + (jump - plan.low) * count :][:count]:
            tall = out.shape[2]
            there = pl.ds(pl.multiple_of(start, tall), tall)
            out[0, 0], out[0, 1] = field[0, there], field[1, there]
            start += tall


def taken(array, rows, start, picks, pick):
    lead = (pl.squeezed,) * (array.ndim - 4)
    return pl.BlockSpec(lead + (picks, 2, rows, LANES), lambda g: (0,) * len(lead) + (pick(g), 0, start, 0))


def column_pass(plan, part, waves, slices, blocks):
    side = plan.length // RADIX
    picks = len(plan.parts[part])
    chunks, merged = plan.sends[part]
    flat = [array for cases in slices for array in cases]
    slice_spec = pl.BlockSpec((plan.group, 2, plan.rows, LANES), lambda g: (0, 0, 0, 0))
    return pl.pallas_call(
        functools.partial(column_kernel, plan, [len(cases) for cases in slices], merged),
        grid=(picks,),
        out_shape=shapes(plan, picks, chunks, merged, SPARE),
        in_specs=[taken(array, plan.rows, 0, pl.squeezed, lambda g, at=at: at) for of in waves for array, at in of]
        + [slice_spec] * len(flat)
        + [pl.BlockSpec((RADIX, 2, 2, side, side), lambda g: (0, 0, 0, 0, 0))],
        out_specs=outputs(
            plan,
            chunks,
            merged,
            lambda rows: pl.BlockSpec((1, 2, rows, LANES), lambda g: (g, 0, 0, 0)),
            lambda rows: pl.BlockSpec((plan.low, 1, 2, rows, LANES), lambda g: (0, g, 0, 0, 0)),
            lambda rows: pl.BlockSpec((1, 2, rows, LANES), lambda g: (g, 0, 0, 0)),
        ),
        scratch_shapes=[
            pltpu.VMEM((2, plan.length, LANES), f32),
            pltpu.VMEM((RADIX, side, 2 * LANES), bf16),
            pltpu.VMEM((RADIX, side, 2 * LANES), bf16),
            pltpu.VMEM((RADIX, side, 2 * LANES), f32),
        ],
        compiler_params=pltpu.CompilerParams(vmem_limit_bytes=VMEM),
        cost_estimate=pl.CostEstimate(flops=0, bytes_accessed=1024, transcendentals=0),
        name=f"column_pass_{part}",
    )(*[array for of in waves for array, _ in of], *flat, blocks)


def row_kernel(plan, chunk, *refs):
    n = plan.group
    ins, blocks, out = refs[: len(plan.parts) * n], refs[len(plan.parts) * n], refs[-9]
    field, d, x, y, staged, in_sems, d_sem, out_sems = refs[-8:]
    me, dist = lax.axis_index("rows"), lax.axis_index("dist")
    side, tall = plan.length // RADIX, plan.chunks[chunk]
    first = sum(plan.chunks[:chunk])
    group = tall // GROUPS
    loads = [[] for _ in range(GROUPS)]
    for r in range(GROUPS):
        here = pl.ds(r * group, group)
        for part, picks in enumerate(plan.parts):
            for jump in range(n):
                array = ins[part * n + jump]
                start = r * group + (0 if array.shape[-2] == tall else first)
                array = array.at[0] if len(array.shape) > 4 else array
                for g, pick in enumerate(picks):
                    unit = plan.unit(jnp.bitwise_xor(me, jump), dist, pick)
                    sem = in_sems.at[r, len(loads[r])]
                    loads[r].append(pltpu.make_async_copy(array.at[g, :, pl.ds(start, group)], field.at[unit, :, here], sem))
    load_blocks = pltpu.make_async_copy(blocks, d, d_sem)
    load_blocks.start()
    for load in loads[0]:
        load.start()
    for of in loads[1:]:
        for load in of:
            load.start()
    wide = side // LANES

    for r in range(GROUPS):
        for load in loads[r]:
            load.wait()

        @pl.loop(0, group // ROW_STRIP)
        def _(s, r=r):
            here = pl.ds(pl.multiple_of(r * group + s * ROW_STRIP, ROW_STRIP), ROW_STRIP)
            line = lambda b, c: jnp.concatenate([field[b * wide + v, c, here] for v in range(wide)], axis=1)
            for k, z in enumerate(dft8([(line(b, 0), line(b, 1)) for b in range(RADIX)], -1)):
                for c in range(2):
                    x[k, 0, c, here], x[k, 1, c, here] = split(z[c])

    load_blocks.wait()

    for k in range(RADIX):
        back = (RADIX - k) % RADIX
        both = x[k].reshape(4 * tall, side)
        high = both[: 2 * tall]

        def by(c):
            product = jnp.dot(both, d[back, c, 0], preferred_element_type=f32)
            return product[: 2 * tall] + product[2 * tall :] + jnp.dot(high, d[back, c, 1], preferred_element_type=f32)

        by_re, by_im = by(0), by(1)
        y[k, 0] = by_re[:tall] - by_im[tall:]
        y[k, 1] = by_re[tall:] + by_im[:tall]

    stores = []
    for r in range(GROUPS):

        @pl.loop(0, group // ROW_STRIP)
        def _(s, r=r):
            here = pl.ds(pl.multiple_of(r * group + s * ROW_STRIP, ROW_STRIP), ROW_STRIP)
            for b, z in enumerate(dft8([(y[k, 0, here], y[k, 1, here]) for k in range(RADIX)], 1)):
                staged[0, here, b * side : (b + 1) * side], staged[1, here, b * side : (b + 1) * side] = z

        stores.append(
            pltpu.make_async_copy(
                staged.at[:, pl.ds(r * group, group)], out.at[0, :, pl.ds(first + r * group, group)], out_sems.at[r]
            )
        )
        stores[-1].start()
    for store in stores:
        store.wait()


def row_pass(plan, chunk, ins, blocks, result):
    side, tall = plan.length // RADIX, plan.chunks[chunk]
    operands = [array for of in ins for array in of] + [blocks]
    aliases = {}
    if result is not None:
        operands.append(result)
        aliases = {len(operands) - 1: 0}
    return pl.pallas_call(
        functools.partial(row_kernel, plan, chunk),
        out_shape=jax.ShapeDtypeStruct((1, 2, plan.rows, plan.length), f32),
        in_specs=[pl.BlockSpec(memory_space=pl.ANY)] * len(operands),
        out_specs=pl.BlockSpec(memory_space=pltpu.HBM),
        scratch_shapes=[
            pltpu.VMEM((plan.units, 2, tall, LANES), f32),
            pltpu.VMEM((RADIX, 2, 2, side, side), bf16),
            pltpu.VMEM((RADIX, 2, 2, tall, side), bf16),
            pltpu.VMEM((RADIX, 2, tall, side), f32),
            pltpu.VMEM((2, tall, plan.length), f32),
            pltpu.SemaphoreType.DMA((GROUPS, plan.units)),
            pltpu.SemaphoreType.DMA,
            pltpu.SemaphoreType.DMA((GROUPS,)),
        ],
        input_output_aliases=aliases,
        compiler_params=pltpu.CompilerParams(vmem_limit_bytes=VMEM),
        cost_estimate=pl.CostEstimate(flops=6 * MIB * 1024 * tall // plan.rows, bytes_accessed=20 * MIB * tall // plan.rows, transcendentals=0),
        name=f"row_pass_{chunk}",
    )(*operands)


def jumped(array, axis, jump):
    return lax.ppermute(array, axis, [(i, i ^ jump) for i in range(lax.axis_size(axis))])


def pick(which, cases):
    return cases[0] if len(cases) == 1 else lax.select_n(which, *cases) if len(cases) > 2 else jnp.where(which == 0, *cases)


def after(array, *others):
    return lax.optimization_barrier((array, *others))[0]


def piece_of(object_slice, place, plan):
    width = object_slice.shape[2] // plan.high
    return lax.dynamic_slice_in_dim(object_slice, place // plan.low * width, width, 2)


def owned(plan, object_slice):
    me = lax.axis_index("rows")
    blocks = [piece_of(object_slice, jnp.bitwise_xor(me, h * 2), plan) for h in range(plan.high)]
    held = [blocks[0]]
    for jump in range(1, plan.group):
        pairs = [
            (d * plan.group + (i ^ jump), d * plan.group + i)
            for d in range(plan.dists)
            for i in range(plan.group)
            if i % 2 == d % 2
        ]
        held.append(lax.ppermute(blocks[jump // 2], ("dist", "rows"), pairs))
    return held


def owners_round(plan, through, blocks, first):
    group, dists = plan.group, plan.dists
    lines = lambda to: [(d * group + i, to(d) * group + i) for d in range(dists) for i in range(group) if i % 2 == d % 2]
    both = ("dist", "rows")
    mine, last = [through], []
    for g in range(1, plan.picks):
        mine.append(lax.ppermute(mine[-1], both, lines(lambda d: (d + 2) % dists)))
    for g in range(plan.picks):
        held = after(mine[g], blocks, first, *last) if g else through
        last = [lax.ppermute(held, both, lines(lambda d: d ^ 1))]
        wait = yield [held, last[0]]
        last += wait or []


def spread(plan, through):
    me, dist = lax.axis_index("rows"), lax.axis_index("dist")
    pieces = lax.all_gather(through, "dist")
    found = []
    for g in range(plan.picks):
        first = lax.rem(dist // plan.low + (plan.picks - g), plan.picks) * plan.low
        parts = []
        for l in range(plan.low):
            block = lax.dynamic_index_in_dim(pieces, first + jnp.bitwise_xor(me % plan.low, l), keepdims=False)
            parts.append(jumped(block, "rows", l) if l else block)
        found.append([jnp.stack(parts, 1).reshape((plan.group,) + through.shape[1:])])
    return found


def sent_far(plan, outs, ahead=()):
    return [jumped(after(block, *ahead), "rows", h * plan.low) for h, block in enumerate(outs[plan.low :], 1)]


def sent_near(plan, outs):
    return [jumped(block, "rows", l) if l else block for l, block in enumerate(outs[: plan.low])]


def sent_on(plan, far, ahead=()):
    got = []
    for block in far:
        got.append(block)
        onward = after(block, *ahead)
        got += [jumped(onward[l], "rows", l) for l in range(1, plan.low)]
    return got


def body(wave, object_slice, fresnel):
    plan = Plan(wave)
    group, high, low = plan.group, plan.high, plan.low
    me = lax.axis_index("rows")

    if low == 2:
        held = owned(plan, object_slice)
    else:
        held = [piece_of(object_slice, jnp.bitwise_xor(me, h * low), plan) for h in range(high)]
        held = [jumped(block, "rows", h * low) if h else block for h, block in enumerate(held)]

    packed = pack(plan, wave)
    held[0] = after(held[0], *[block for blocks in packed for block in blocks])
    sent = [sent_near(plan, outs) + sent_on(plan, sent_far(plan, outs)) for outs in packed]
    waves = [[(array, at) for array in got] for got, picks in zip(sent, plan.batches) for at in range(len(picks))]

    through = transmission(held)
    blocks = circulant_blocks(after(fresnel, through), plan.length)
    rounds = owners_round(plan, through, blocks, sent[0][low]) if low == 2 else iter(spread(plan, through))

    gone, slices, last = [], [], len(plan.parts) - 1
    for part, picks in enumerate(plan.parts):
        while len(slices) <= picks[-1]:
            wait = [sent[-1][low], outs[0]] if low == 2 and len(slices) == 2 else None
            slices.append(rounds.send(wait) if wait else next(rounds))
        here = slice(picks[0], picks[-1] + 1)
        if part and part == last:
            gone[0] += sent_on(plan, flown, outs[:1])
            blocks = after(blocks, *gone[0], *gone[1][:low])
        outs = column_pass(plan, part, waves[here], slices[here], blocks)
        gone.append(sent_near(plan, outs))
        if part == 0:
            flown = sent_far(plan, outs, [sent[-1][j] for j in range(low, group, low)] if last else [])
        elif part < last:
            gone[-1] += [jumped(block, "rows", j) for j, block in enumerate(outs[low:], low)]
    result, count = None, len(plan.chunks)
    if not last:
        gone[0] += sent_on(plan, flown)
    for chunk in range(count):
        ins = list(gone)
        if last:
            far = [outs[low + (j - low) * count + chunk] for j in range(low, group)]
            ins[-1] = gone[-1] + [jumped(block, "rows", j) for j, block in enumerate(far, low)]
        result = row_pass(plan, chunk, ins, blocks, result)
    return result


def solution(mesh):
    return jax.shard_map(
        body,
        mesh=mesh,
        in_specs=(P("dist", None, "rows", None), P(None, "rows", "dist"), P("dist")),
        out_specs=P("dist", None, "rows", None),
        check_vma=False,
    )
```

```python
import functools
import math

import jax
import jax.numpy as jnp
import numpy as np
from jax import lax
from jax.experimental import pallas as pl
from jax.experimental.pallas import tpu as pltpu
from jax.sharding import PartitionSpec as P

f32, bf16 = jnp.float32, jnp.bfloat16
LANES = 128
RADIX = 8
STRIP = 32
ROW_STRIP = 16
GROUPS = 4
SPARE = 8
MIB = 1 << 20
VMEM = 64 * MIB - 256 * 1024
EARLY_VMEM = 56 * MIB
ROOT = math.sqrt(0.5)


def turn(z, quarter):
    re, im = z
    return ((re, im), (-im, re), (-re, -im), (im, -re))[quarter % 4]


def plus(a, b):
    return (a[0] + b[0], a[1] + b[1])


def minus(a, b):
    return (a[0] - b[0], a[1] - b[1])


def dft4(z, sign):
    even, odd = plus(z[0], z[2]), plus(z[1], z[3])
    low, high = minus(z[0], z[2]), turn(minus(z[1], z[3]), sign)
    return [plus(even, odd), plus(low, high), minus(even, odd), minus(low, high)]


def dft8(z, sign):
    even, odd = dft4(z[0::2], sign), dft4(z[1::2], sign)
    (re1, im1), (re3, im3) = odd[1], odd[3]
    odd[1] = (ROOT * (re1 - sign * im1), ROOT * (im1 + sign * re1))
    odd[2] = turn(odd[2], sign)
    odd[3] = (-ROOT * (re3 + sign * im3), ROOT * (sign * re3 - im3))
    return [plus(a, b) for a, b in zip(even, odd)] + [minus(a, b) for a, b in zip(even, odd)]


def split(value):
    high = value.astype(bf16)
    return high, (value - high.astype(f32)).astype(bf16)


def dot3(a_high, a_low, b_high, b_low):
    dot = functools.partial(jnp.dot, preferred_element_type=f32)
    return dot(a_high, b_high) + (dot(a_high, b_low) + dot(a_low, b_high))


def blocks_kernel(response, wheel, right, twist, blocks):
    half = wheel.shape[1]
    k = pl.program_id(0)
    h_re, h_im = response[0, pl.ds(k, 1)], response[1, pl.ds(k, 1)]
    w_re, w_im = wheel[0], wheel[1]
    left = jnp.concatenate((w_re * h_re - w_im * h_im, w_re * h_im + w_im * h_re), axis=1)
    both = jnp.dot(left, right[...], precision=lax.Precision.HIGHEST, preferred_element_type=f32)
    both_re, both_im = both[:, :half], both[:, half:]
    t_re, t_im = twist[0, 0], twist[0, 1]
    high, low = split(both_re * t_re - both_im * t_im)
    blocks[0, 0, 0], blocks[0, 0, 1] = high, low
    high, low = split(both_re * t_im + both_im * t_re)
    blocks[0, 1, 0], blocks[0, 1, 1] = high, low


def circulant_blocks(fresnel, length):
    side = length // RADIX
    index = np.arange(RADIX)[:, None] + RADIX * np.arange(side)[None]
    freq = np.where(index < length // 2, index, index - length).astype(np.float32) / length
    phase = (-math.pi * fresnel[0]) * (freq * freq)
    response = jnp.stack((jnp.cos(phase), jnp.sin(phase)))
    line = np.arange(side)
    angle = 2 * np.pi / side * (line[:, None] * line[None] % side)
    wheel = np.stack((np.cos(angle), np.sin(angle))).astype(np.float32)
    scale = 1.0 / (side * RADIX)
    w_re, w_im = np.cos(angle).T * scale, np.sin(angle).T * scale
    right = np.block([[w_re, -w_im], [w_im, w_re]]).astype(np.float32)
    apart = np.arange(RADIX)[:, None, None] * (line[:, None] - line[None])
    twist = np.stack((np.cos(2 * np.pi / length * apart), np.sin(2 * np.pi / length * apart)), 1).astype(np.float32)
    whole = lambda *shape: pl.BlockSpec(shape, lambda k: (0,) * len(shape))
    return pl.pallas_call(
        blocks_kernel,
        grid=(RADIX,),
        out_shape=jax.ShapeDtypeStruct((RADIX, 2, 2, side, side), bf16),
        in_specs=[
            whole(2, RADIX, side),
            whole(2, side, side),
            whole(2 * side, 2 * side),
            pl.BlockSpec((1, 2, side, side), lambda k: (k, 0, 0, 0)),
        ],
        out_specs=pl.BlockSpec((1, 2, 2, side, side), lambda k: (k, 0, 0, 0, 0)),
        compiler_params=pltpu.CompilerParams(vmem_limit_bytes=EARLY_VMEM),
        name="circulant_blocks",
    )(response, jnp.asarray(wheel), jnp.asarray(right), jnp.asarray(twist))


class Plan:
    def __init__(self, wave):
        self.group, self.dists = lax.axis_size("rows"), lax.axis_size("dist")
        self.rows, self.length = wave.shape[2], wave.shape[3]
        self.units = self.length // LANES
        self.high = min(self.units // self.dists, self.group)
        self.low = self.group // self.high
        self.picks = self.dists // self.low
        halves = self.picks == 4
        self.batches = [[0, 1], [2, 3]] if halves else [list(range(self.picks))]
        self.parts = [[0, 1], [2], [3]] if halves else [list(range(self.picks))]
        self.chunks = [self.rows // 2] * 2 if halves and self.rows // 4 >= LANES else [self.rows]
        self.sends = [([self.rows], True), ([self.rows], False), (self.chunks, False)] if halves else [([self.rows], True)]
        self.order = sorted(range(self.group), key=lambda jump: (-(jump // self.low), jump % self.low))

    def guest(self):
        return jnp.bitwise_xor(lax.axis_index("rows") % self.low, lax.axis_index("dist") % self.low)

    def unit(self, place, dist, pick):
        other = lax.rem(dist // self.low + (self.picks - pick), self.picks) * self.low + place % self.low
        return other * self.high + place // self.low


def outputs(plan, chunks, merged, near, far, direct):
    nears = [near(plan.rows) for _ in range(plan.low)]
    if merged:
        return nears + [far(plan.rows) for _ in range(plan.high - 1)]
    return nears + [direct(rows) for _ in range(plan.low, plan.group) for rows in chunks]


def shapes(plan, picks, chunks, merged, spare=0):
    shape = lambda *dims: jax.ShapeDtypeStruct(dims, f32)
    return outputs(
        plan,
        chunks,
        merged,
        lambda rows: shape(picks, 2, rows, LANES),
        lambda rows: shape(plan.low, picks, 2, rows + spare, LANES),
        lambda rows: shape(picks, 2, rows + (spare if rows == plan.rows else 0), LANES),
    )


def target(plan, outs, jump):
    high, low = jump // plan.low, jump % plan.low
    return outs[plan.low + high - 1].at[low] if high else outs[low]


def pack_kernel(plan, wave, *refs):
    outs, (staged, ins, sems) = refs[:-3], refs[-3:]
    me, dist = lax.axis_index("rows"), lax.axis_index("dist")
    size = len(outs) // len(plan.batches)
    loads, stores = [], []
    for batch, picks in enumerate(plan.batches):
        for jump in plan.order:
            for at, pick in enumerate(picks):
                slot = len(loads)
                unit = plan.unit(jnp.bitwise_xor(me, jump), dist, pick)
                start = pl.multiple_of(unit * LANES, LANES)
                out = target(plan, outs[batch * size : (batch + 1) * size], jump).at[at, :, pl.ds(0, plan.rows)]
                loads.append(pltpu.make_async_copy(wave.at[0, :, :, pl.ds(start, LANES)], staged.at[slot], ins.at[slot]))
                stores.append(pltpu.make_async_copy(staged.at[slot], out, sems.at[slot]))
    for load in loads:
        load.start()
    for load, store in zip(loads, stores):
        load.wait()
        store.start()
    for store in stores:
        store.wait()


def pack(plan, wave):
    outs = [shape for picks in plan.batches for shape in shapes(plan, len(picks), [plan.rows], True, SPARE)]
    hbm = pl.BlockSpec(memory_space=pltpu.HBM)
    outs = pl.pallas_call(
        functools.partial(pack_kernel, plan),
        out_shape=outs,
        in_specs=[hbm],
        out_specs=[hbm] * len(outs),
        scratch_shapes=[
            pltpu.VMEM((plan.units, 2, plan.rows, LANES), f32),
            pltpu.SemaphoreType.DMA((plan.units,)),
            pltpu.SemaphoreType.DMA((plan.units,)),
        ],
        compiler_params=pltpu.CompilerParams(vmem_limit_bytes=EARLY_VMEM),
        cost_estimate=pl.CostEstimate(flops=0, bytes_accessed=16 * MIB, transcendentals=0),
        name="pack",
    )(wave)
    size = len(outs) // len(plan.batches)
    return [outs[batch * size : (batch + 1) * size] for batch in range(len(plan.batches))]


def series(square, first, count):
    total = jnp.ones_like(square)
    for i in reversed(range(count)):
        total = 1.0 - square * (1.0 / ((first + 2 * i) * (first + 2 * i + 1))) * total
    return total


def transmission_kernel(*refs):
    out = refs[-1]
    for h, piece in enumerate(refs[:-1]):
        amplitude, square = jnp.exp(-piece[1]), piece[0] * piece[0]
        out[h, 0] = amplitude * series(square, 1, 7)
        out[h, 1] = amplitude * (piece[0] * series(square, 2, 7))


def transmission(held):
    rows = held[0].shape[1]
    tall = min(rows, LANES)
    return pl.pallas_call(
        transmission_kernel,
        grid=(rows // tall,),
        out_shape=jax.ShapeDtypeStruct((len(held),) + held[0].shape, f32),
        in_specs=[pl.BlockSpec((2, tall, LANES), lambda s: (0, s, 0))] * len(held),
        out_specs=pl.BlockSpec((len(held), 2, tall, LANES), lambda s: (0, 0, s, 0)),
        compiler_params=pltpu.CompilerParams(vmem_limit_bytes=EARLY_VMEM),
        name="transmission",
    )(*held)


def column_kernel(plan, counts, merged, *refs):
    n = plan.group
    waves, refs = [refs[g * n : (g + 1) * n] for g in range(len(counts))], refs[len(counts) * n :]
    slices = []
    for count in counts:
        slices.append(refs[:count])
        refs = refs[count:]
    blocks, outs = refs[0], refs[1:-6]
    field, x_high, x_low, y, held, sems = refs[-6:]
    me, step = lax.axis_index("rows"), pl.program_id(0)
    load = lambda g, case: pltpu.make_async_copy(slices[g][case], held.at[g], sems.at[g])

    @pl.when(step == 0)
    def _():
        for g, cases in enumerate(slices):
            for case in range(len(cases)):
                @pl.when(plan.guest() % len(cases) == case)
                def _(g=g, case=case):
                    load(g, case).start()

    for g in range(len(counts)):

        @pl.when(step == g)
        def _(g=g):
            load(g, 0).wait()

    rows, side = plan.rows, plan.length // RADIX
    for g in range(len(counts)):
        for jump in range(n):

            @pl.when(step == g)
            def _(g=g, jump=jump):
                base = jnp.bitwise_xor(me, jump) * rows

                @pl.loop(0, rows // STRIP)
                def _(s):
                    here = pl.ds(pl.multiple_of(s * STRIP, STRIP), STRIP)
                    t_re, t_im = held[g, jump, 0, here], held[g, jump, 1, here]
                    w_re, w_im = waves[g][jump][0, here], waves[g][jump][1, here]
                    there = pl.ds(pl.multiple_of(base + s * STRIP, STRIP), STRIP)
                    field[0, there] = w_re * t_re - w_im * t_im
                    field[1, there] = w_re * t_im + w_im * t_re

    @pl.loop(0, side // STRIP)
    def _(s):
        at = lambda b: pl.ds(pl.multiple_of(b * side + s * STRIP, STRIP), STRIP)
        here = pl.ds(pl.multiple_of(s * STRIP, STRIP), STRIP)
        for k, z in enumerate(dft8([(field[0, at(b)], field[1, at(b)]) for b in range(RADIX)], -1)):
            x_high[k, here], x_low[k, here] = split(jnp.concatenate(z, axis=1))

    @pl.loop(0, RADIX)
    def _(k):
        by_re = dot3(blocks[k, 0, 0], blocks[k, 0, 1], x_high[k], x_low[k])
        by_im = dot3(blocks[k, 1, 0], blocks[k, 1, 1], x_high[k], x_low[k])
        y[k, :, :LANES] = by_re[:, :LANES] - by_im[:, LANES:]
        y[k, :, LANES:] = by_re[:, LANES:] + by_im[:, :LANES]

    @pl.loop(0, side // STRIP)
    def _(s):
        here = pl.ds(pl.multiple_of(s * STRIP, STRIP), STRIP)
        for b, z in enumerate(dft8([(y[k, here, :LANES], y[k, here, LANES:]) for k in range(RADIX)], 1)):
            there = pl.ds(pl.multiple_of(b * side + s * STRIP, STRIP), STRIP)
            field[0, there], field[1, there] = z

    for jump in range(n):
        start = jnp.bitwise_xor(me, jump) * rows
        if jump < plan.low or merged:
            there = pl.ds(pl.multiple_of(start, rows), rows)
            out = target(plan, outs, jump)
            out[0, 0], out[0, 1] = field[0, there], field[1, there]
            continue
        count = (len(outs) - plan.low) // (n - plan.low)
        for out in outs[plan.low + (jump - plan.low) * count :][:count]:
            tall = out.shape[2]
            there = pl.ds(pl.multiple_of(start, tall), tall)
            out[0, 0], out[0, 1] = field[0, there], field[1, there]
            start += tall


def taken(array, rows, start, picks, pick):
    lead = (pl.squeezed,) * (array.ndim - 4)
    return pl.BlockSpec(lead + (picks, 2, rows, LANES), lambda g: (0,) * len(lead) + (pick(g), 0, start, 0))


def column_pass(plan, part, waves, slices, blocks):
    side = plan.length // RADIX
    picks = len(plan.parts[part])
    chunks, merged = plan.sends[part]
    flat = [array for cases in slices for array in cases]
    return pl.pallas_call(
        functools.partial(column_kernel, plan, [len(cases) for cases in slices], merged),
        grid=(picks,),
        out_shape=shapes(plan, picks, chunks, merged, SPARE),
        in_specs=[taken(array, plan.rows, 0, pl.squeezed, lambda g, at=at: at) for of in waves for array, at in of]
        + [pl.BlockSpec(memory_space=pl.ANY)] * len(flat)
        + [pl.BlockSpec((RADIX, 2, 2, side, side), lambda g: (0, 0, 0, 0, 0))],
        out_specs=outputs(
            plan,
            chunks,
            merged,
            lambda rows: pl.BlockSpec((1, 2, rows, LANES), lambda g: (g, 0, 0, 0)),
            lambda rows: pl.BlockSpec((plan.low, 1, 2, rows, LANES), lambda g: (0, g, 0, 0, 0)),
            lambda rows: pl.BlockSpec((1, 2, rows, LANES), lambda g: (g, 0, 0, 0)),
        ),
        scratch_shapes=[
            pltpu.VMEM((2, plan.length, LANES), f32),
            pltpu.VMEM((RADIX, side, 2 * LANES), bf16),
            pltpu.VMEM((RADIX, side, 2 * LANES), bf16),
            pltpu.VMEM((RADIX, side, 2 * LANES), f32),
            pltpu.VMEM((picks, plan.group, 2, plan.rows, LANES), f32),
            pltpu.SemaphoreType.DMA((picks,)),
        ],
        compiler_params=pltpu.CompilerParams(vmem_limit_bytes=VMEM),
        cost_estimate=pl.CostEstimate(flops=0, bytes_accessed=1024, transcendentals=0),
        name=f"column_pass_{part}",
    )(*[array for of in waves for array, _ in of], *flat, blocks)


def row_kernel(plan, chunk, *refs):
    n = plan.group
    ins, blocks, out = refs[: len(plan.parts) * n], refs[len(plan.parts) * n], refs[-9]
    field, d, x, y, staged, in_sems, d_sem, out_sems = refs[-8:]
    me, dist = lax.axis_index("rows"), lax.axis_index("dist")
    side, tall = plan.length // RADIX, plan.chunks[chunk]
    first = sum(plan.chunks[:chunk])
    group = tall // GROUPS
    loads = [[] for _ in range(GROUPS)]
    for r in range(GROUPS):
        here = pl.ds(r * group, group)
        for part, picks in enumerate(plan.parts):
            for jump in range(n):
                array = ins[part * n + jump]
                start = r * group + (0 if array.shape[-2] == tall else first)
                array = array.at[0] if len(array.shape) > 4 else array
                for g, pick in enumerate(picks):
                    unit = plan.unit(jnp.bitwise_xor(me, jump), dist, pick)
                    sem = in_sems.at[r, len(loads[r])]
                    loads[r].append(pltpu.make_async_copy(array.at[g, :, pl.ds(start, group)], field.at[unit, :, here], sem))
    load_blocks = pltpu.make_async_copy(blocks, d, d_sem)
    load_blocks.start()
    for load in loads[0]:
        load.start()
    for of in loads[1:]:
        for load in of:
            load.start()
    wide = side // LANES

    for r in range(GROUPS):
        for load in loads[r]:
            load.wait()

        @pl.loop(0, group // ROW_STRIP)
        def _(s, r=r):
            here = pl.ds(pl.multiple_of(r * group + s * ROW_STRIP, ROW_STRIP), ROW_STRIP)
            line = lambda b, c: jnp.concatenate([field[b * wide + v, c, here] for v in range(wide)], axis=1)
            for k, z in enumerate(dft8([(line(b, 0), line(b, 1)) for b in range(RADIX)], -1)):
                for c in range(2):
                    x[k, 0, c, here], x[k, 1, c, here] = split(z[c])

    load_blocks.wait()

    for k in range(RADIX):
        back = (RADIX - k) % RADIX
        both = x[k].reshape(4 * tall, side)
        high = both[: 2 * tall]

        def by(c):
            product = jnp.dot(both, d[back, c, 0], preferred_element_type=f32)
            return product[: 2 * tall] + product[2 * tall :] + jnp.dot(high, d[back, c, 1], preferred_element_type=f32)

        by_re, by_im = by(0), by(1)
        y[k, 0] = by_re[:tall] - by_im[tall:]
        y[k, 1] = by_re[tall:] + by_im[:tall]

    stores = []
    for r in range(GROUPS):

        @pl.loop(0, group // ROW_STRIP)
        def _(s, r=r):
            here = pl.ds(pl.multiple_of(r * group + s * ROW_STRIP, ROW_STRIP), ROW_STRIP)
            for b, z in enumerate(dft8([(y[k, 0, here], y[k, 1, here]) for k in range(RADIX)], 1)):
                staged[0, here, b * side : (b + 1) * side], staged[1, here, b * side : (b + 1) * side] = z

        stores.append(
            pltpu.make_async_copy(
                staged.at[:, pl.ds(r * group, group)], out.at[0, :, pl.ds(first + r * group, group)], out_sems.at[r]
            )
        )
        stores[-1].start()
    for store in stores:
        store.wait()


def row_pass(plan, chunk, ins, blocks, result):
    side, tall = plan.length // RADIX, plan.chunks[chunk]
    operands = [array for of in ins for array in of] + [blocks]
    aliases = {}
    if result is not None:
        operands.append(result)
        aliases = {len(operands) - 1: 0}
    return pl.pallas_call(
        functools.partial(row_kernel, plan, chunk),
        out_shape=jax.ShapeDtypeStruct((1, 2, plan.rows, plan.length), f32),
        in_specs=[pl.BlockSpec(memory_space=pl.ANY)] * len(operands),
        out_specs=pl.BlockSpec(memory_space=pltpu.HBM),
        scratch_shapes=[
            pltpu.VMEM((plan.units, 2, tall, LANES), f32),
            pltpu.VMEM((RADIX, 2, 2, side, side), bf16),
            pltpu.VMEM((RADIX, 2, 2, tall, side), bf16),
            pltpu.VMEM((RADIX, 2, tall, side), f32),
            pltpu.VMEM((2, tall, plan.length), f32),
            pltpu.SemaphoreType.DMA((GROUPS, plan.units)),
            pltpu.SemaphoreType.DMA,
            pltpu.SemaphoreType.DMA((GROUPS,)),
        ],
        input_output_aliases=aliases,
        compiler_params=pltpu.CompilerParams(vmem_limit_bytes=VMEM),
        cost_estimate=pl.CostEstimate(flops=6 * MIB * 1024 * tall // plan.rows, bytes_accessed=20 * MIB * tall // plan.rows, transcendentals=0),
        name=f"row_pass_{chunk}",
    )(*operands)


def jumped(array, axis, jump):
    return lax.ppermute(array, axis, [(i, i ^ jump) for i in range(lax.axis_size(axis))])


def pick(which, cases):
    return cases[0] if len(cases) == 1 else lax.select_n(which, *cases) if len(cases) > 2 else jnp.where(which == 0, *cases)


def after(array, *others):
    return lax.optimization_barrier((array, *others))[0]


def piece_of(object_slice, place, plan):
    width = object_slice.shape[2] // plan.high
    return lax.dynamic_slice_in_dim(object_slice, place // plan.low * width, width, 2)


def owned(plan, object_slice):
    me = lax.axis_index("rows")
    blocks = [piece_of(object_slice, jnp.bitwise_xor(me, h * 2), plan) for h in range(plan.high)]
    held = [blocks[0]]
    for jump in range(1, plan.group):
        pairs = [
            (d * plan.group + (i ^ jump), d * plan.group + i)
            for d in range(plan.dists)
            for i in range(plan.group)
            if i % 2 == d % 2
        ]
        held.append(lax.ppermute(blocks[jump // 2], ("dist", "rows"), pairs))
    return held


def owners_round(plan, through, blocks, first):
    group, dists = plan.group, plan.dists
    lines = lambda to: [(d * group + i, to(d) * group + i) for d in range(dists) for i in range(group) if i % 2 == d % 2]
    both = ("dist", "rows")
    mine, last = [through], []
    for g in range(1, plan.picks):
        mine.append(lax.ppermute(mine[-1], both, lines(lambda d: (d + 2) % dists)))
    for g in range(plan.picks):
        held = after(mine[g], blocks, first, *last) if g else through
        last = [lax.ppermute(held, both, lines(lambda d: d ^ 1))]
        wait = yield [held, last[0]]
        last += wait or []


def spread(plan, through):
    me, dist = lax.axis_index("rows"), lax.axis_index("dist")
    pieces = lax.all_gather(through, "dist")
    found = []
    for g in range(plan.picks):
        first = lax.rem(dist // plan.low + (plan.picks - g), plan.picks) * plan.low
        parts = []
        for l in range(plan.low):
            block = lax.dynamic_index_in_dim(pieces, first + jnp.bitwise_xor(me % plan.low, l), keepdims=False)
            parts.append(jumped(block, "rows", l) if l else block)
        found.append([jnp.stack(parts, 1).reshape((plan.group,) + through.shape[1:])])
    return found


def sent_far(plan, outs, ahead=()):
    return [jumped(after(block, *ahead), "rows", h * plan.low) for h, block in enumerate(outs[plan.low :], 1)]


def sent_near(plan, outs):
    return [jumped(block, "rows", l) if l else block for l, block in enumerate(outs[: plan.low])]


def sent_on(plan, far, ahead=()):
    got = []
    for block in far:
        got.append(block)
        onward = after(block, *ahead)
        got += [jumped(onward[l], "rows", l) for l in range(1, plan.low)]
    return got


def body(wave, object_slice, fresnel):
    plan = Plan(wave)
    group, high, low = plan.group, plan.high, plan.low
    me = lax.axis_index("rows")

    if low == 2:
        held = owned(plan, object_slice)
    else:
        held = [piece_of(object_slice, jnp.bitwise_xor(me, h * low), plan) for h in range(high)]
        held = [jumped(block, "rows", h * low) if h else block for h, block in enumerate(held)]

    packed = pack(plan, wave)
    held[0] = after(held[0], *[block for blocks in packed for block in blocks])
    sent = [sent_near(plan, outs) + sent_on(plan, sent_far(plan, outs)) for outs in packed]
    waves = [[(array, at) for array in got] for got, picks in zip(sent, plan.batches) for at in range(len(picks))]

    through = transmission(held)
    blocks = circulant_blocks(after(fresnel, through), plan.length)
    rounds = owners_round(plan, through, blocks, sent[0][low]) if low == 2 else iter(spread(plan, through))

    gone, slices, last = [], [], len(plan.parts) - 1
    for part, picks in enumerate(plan.parts):
        while len(slices) <= picks[-1]:
            wait = [sent[-1][low], outs[0]] if low == 2 and len(slices) == 2 else None
            slices.append(rounds.send(wait) if wait else next(rounds))
        here = slice(picks[0], picks[-1] + 1)
        if part and part == last:
            gone[0] += sent_on(plan, flown, outs[:1])
            blocks = after(blocks, *gone[0], *gone[1][:low])
        outs = column_pass(plan, part, waves[here], slices[here], blocks)
        gone.append(sent_near(plan, outs))
        if part == 0:
            flown = sent_far(plan, outs, [sent[-1][j] for j in range(low, group, low)] if last else [])
        elif part < last:
            gone[-1] += [jumped(block, "rows", j) for j, block in enumerate(outs[low:], low)]
    result, count = None, len(plan.chunks)
    if not last:
        gone[0] += sent_on(plan, flown)
    for chunk in range(count):
        ins = list(gone)
        if last:
            far = [outs[low + (j - low) * count + chunk] for j in range(low, group)]
            ins[-1] = gone[-1] + [jumped(block, "rows", j) for j, block in enumerate(far, low)]
        result = row_pass(plan, chunk, ins, blocks, result)
    return result


def solution(mesh):
    return jax.shard_map(
        body,
        mesh=mesh,
        in_specs=(P("dist", None, "rows", None), P(None, "rows", "dist"), P("dist")),
        out_specs=P("dist", None, "rows", None),
        check_vma=False,
    )
```

```python
import functools
import math

import jax
import jax.numpy as jnp
import numpy as np
from jax import lax
from jax.experimental import pallas as pl
from jax.experimental.pallas import tpu as pltpu
from jax.sharding import PartitionSpec as P

f32, bf16 = jnp.float32, jnp.bfloat16
LANES = 128
RADIX = 8
STRIP = 32
ROW_STRIP = 16
GROUPS = 8
SPARE = 8
MIB = 1 << 20
VMEM = 64 * MIB - 256 * 1024
EARLY_VMEM = 56 * MIB
ROOT = math.sqrt(0.5)


def turn(z, quarter):
    re, im = z
    return ((re, im), (-im, re), (-re, -im), (im, -re))[quarter % 4]


def plus(a, b):
    return (a[0] + b[0], a[1] + b[1])


def minus(a, b):
    return (a[0] - b[0], a[1] - b[1])


def dft4(z, sign):
    even, odd = plus(z[0], z[2]), plus(z[1], z[3])
    low, high = minus(z[0], z[2]), turn(minus(z[1], z[3]), sign)
    return [plus(even, odd), plus(low, high), minus(even, odd), minus(low, high)]


def dft8(z, sign):
    even, odd = dft4(z[0::2], sign), dft4(z[1::2], sign)
    (re1, im1), (re3, im3) = odd[1], odd[3]
    odd[1] = (ROOT * (re1 - sign * im1), ROOT * (im1 + sign * re1))
    odd[2] = turn(odd[2], sign)
    odd[3] = (-ROOT * (re3 + sign * im3), ROOT * (sign * re3 - im3))
    return [plus(a, b) for a, b in zip(even, odd)] + [minus(a, b) for a, b in zip(even, odd)]


def split(value):
    high = value.astype(bf16)
    return high, (value - high.astype(f32)).astype(bf16)


def dot3(a_high, a_low, b_high, b_low):
    dot = functools.partial(jnp.dot, preferred_element_type=f32)
    return dot(a_high, b_high) + (dot(a_high, b_low) + dot(a_low, b_high))


def blocks_kernel(response, wheel, right, twist, blocks):
    half = wheel.shape[1]
    k = pl.program_id(0)
    h_re, h_im = response[0, pl.ds(k, 1)], response[1, pl.ds(k, 1)]
    w_re, w_im = wheel[0], wheel[1]
    left = jnp.concatenate((w_re * h_re - w_im * h_im, w_re * h_im + w_im * h_re), axis=1)
    both = jnp.dot(left, right[...], precision=lax.Precision.HIGHEST, preferred_element_type=f32)
    both_re, both_im = both[:, :half], both[:, half:]
    t_re, t_im = twist[0, 0], twist[0, 1]
    high, low = split(both_re * t_re - both_im * t_im)
    blocks[0, 0, 0], blocks[0, 0, 1] = high, low
    high, low = split(both_re * t_im + both_im * t_re)
    blocks[0, 1, 0], blocks[0, 1, 1] = high, low


def circulant_blocks(fresnel, length):
    side = length // RADIX
    index = np.arange(RADIX)[:, None] + RADIX * np.arange(side)[None]
    freq = np.where(index < length // 2, index, index - length).astype(np.float32) / length
    phase = (-math.pi * fresnel[0]) * (freq * freq)
    response = jnp.stack((jnp.cos(phase), jnp.sin(phase)))
    line = np.arange(side)
    angle = 2 * np.pi / side * (line[:, None] * line[None] % side)
    wheel = np.stack((np.cos(angle), np.sin(angle))).astype(np.float32)
    scale = 1.0 / (side * RADIX)
    w_re, w_im = np.cos(angle).T * scale, np.sin(angle).T * scale
    right = np.block([[w_re, -w_im], [w_im, w_re]]).astype(np.float32)
    apart = np.arange(RADIX)[:, None, None] * (line[:, None] - line[None])
    twist = np.stack((np.cos(2 * np.pi / length * apart), np.sin(2 * np.pi / length * apart)), 1).astype(np.float32)
    whole = lambda *shape: pl.BlockSpec(shape, lambda k: (0,) * len(shape))
    return pl.pallas_call(
        blocks_kernel,
        grid=(RADIX,),
        out_shape=jax.ShapeDtypeStruct((RADIX, 2, 2, side, side), bf16),
        in_specs=[
            whole(2, RADIX, side),
            whole(2, side, side),
            whole(2 * side, 2 * side),
            pl.BlockSpec((1, 2, side, side), lambda k: (k, 0, 0, 0)),
        ],
        out_specs=pl.BlockSpec((1, 2, 2, side, side), lambda k: (k, 0, 0, 0, 0)),
        compiler_params=pltpu.CompilerParams(vmem_limit_bytes=EARLY_VMEM),
        name="circulant_blocks",
    )(response, jnp.asarray(wheel), jnp.asarray(right), jnp.asarray(twist))


class Plan:
    def __init__(self, wave):
        self.group, self.dists = lax.axis_size("rows"), lax.axis_size("dist")
        self.rows, self.length = wave.shape[2], wave.shape[3]
        self.units = self.length // LANES
        self.high = min(self.units // self.dists, self.group)
        self.low = self.group // self.high
        self.picks = self.dists // self.low
        halves = self.picks == 4
        self.batches = [[0, 1], [2, 3]] if halves else [list(range(self.picks))]
        self.parts = [[0, 1], [2], [3]] if halves else [list(range(self.picks))]
        self.chunks = [self.rows // 2] * 2 if halves and self.rows // 4 >= LANES else [self.rows]
        self.sends = [([self.rows], True), ([self.rows], False), (self.chunks, False)] if halves else [([self.rows], True)]
        self.order = sorted(range(self.group), key=lambda jump: (-(jump // self.low), jump % self.low))

    def guest(self):
        return jnp.bitwise_xor(lax.axis_index("rows") % self.low, lax.axis_index("dist") % self.low)

    def unit(self, place, dist, pick):
        other = lax.rem(dist // self.low + (self.picks - pick), self.picks) * self.low + place % self.low
        return other * self.high + place // self.low


def outputs(plan, chunks, merged, near, far, direct):
    nears = [near(plan.rows) for _ in range(plan.low)]
    if merged:
        return nears + [far(plan.rows) for _ in range(plan.high - 1)]
    return nears + [direct(rows) for _ in range(plan.low, plan.group) for rows in chunks]


def shapes(plan, picks, chunks, merged, spare=0):
    shape = lambda *dims: jax.ShapeDtypeStruct(dims, f32)
    return outputs(
        plan,
        chunks,
        merged,
        lambda rows: shape(picks, 2, rows, LANES),
        lambda rows: shape(plan.low, picks, 2, rows + spare, LANES),
        lambda rows: shape(picks, 2, rows + (spare if rows == plan.rows else 0), LANES),
    )


def target(plan, outs, jump):
    high, low = jump // plan.low, jump % plan.low
    return outs[plan.low + high - 1].at[low] if high else outs[low]


def pack_kernel(plan, wave, *refs):
    outs, (staged, ins, sems) = refs[:-3], refs[-3:]
    me, dist = lax.axis_index("rows"), lax.axis_index("dist")
    size = len(outs) // len(plan.batches)
    loads, stores = [], []
    for batch, picks in enumerate(plan.batches):
        for jump in plan.order:
            for at, pick in enumerate(picks):
                slot = len(loads)
                unit = plan.unit(jnp.bitwise_xor(me, jump), dist, pick)
                start = pl.multiple_of(unit * LANES, LANES)
                out = target(plan, outs[batch * size : (batch + 1) * size], jump).at[at, :, pl.ds(0, plan.rows)]
                loads.append(pltpu.make_async_copy(wave.at[0, :, :, pl.ds(start, LANES)], staged.at[slot], ins.at[slot]))
                stores.append(pltpu.make_async_copy(staged.at[slot], out, sems.at[slot]))
    for load in loads:
        load.start()
    for load, store in zip(loads, stores):
        load.wait()
        store.start()
    for store in stores:
        store.wait()


def pack(plan, wave):
    outs = [shape for picks in plan.batches for shape in shapes(plan, len(picks), [plan.rows], True, SPARE)]
    hbm = pl.BlockSpec(memory_space=pltpu.HBM)
    outs = pl.pallas_call(
        functools.partial(pack_kernel, plan),
        out_shape=outs,
        in_specs=[hbm],
        out_specs=[hbm] * len(outs),
        scratch_shapes=[
            pltpu.VMEM((plan.units, 2, plan.rows, LANES), f32),
            pltpu.SemaphoreType.DMA((plan.units,)),
            pltpu.SemaphoreType.DMA((plan.units,)),
        ],
        compiler_params=pltpu.CompilerParams(vmem_limit_bytes=EARLY_VMEM),
        cost_estimate=pl.CostEstimate(flops=0, bytes_accessed=16 * MIB, transcendentals=0),
        name="pack",
    )(wave)
    size = len(outs) // len(plan.batches)
    return [outs[batch * size : (batch + 1) * size] for batch in range(len(plan.batches))]


def series(square, first, count):
    total = jnp.ones_like(square)
    for i in reversed(range(count)):
        total = 1.0 - square * (1.0 / ((first + 2 * i) * (first + 2 * i + 1))) * total
    return total


def transmission_kernel(*refs):
    out = refs[-1]
    for h, piece in enumerate(refs[:-1]):
        amplitude, square = jnp.exp(-piece[1]), piece[0] * piece[0]
        out[h, 0] = amplitude * series(square, 1, 7)
        out[h, 1] = amplitude * (piece[0] * series(square, 2, 7))


def transmission(held):
    rows = held[0].shape[1]
    tall = min(rows, LANES)
    return pl.pallas_call(
        transmission_kernel,
        grid=(rows // tall,),
        out_shape=jax.ShapeDtypeStruct((len(held),) + held[0].shape, f32),
        in_specs=[pl.BlockSpec((2, tall, LANES), lambda s: (0, s, 0))] * len(held),
        out_specs=pl.BlockSpec((len(held), 2, tall, LANES), lambda s: (0, 0, s, 0)),
        compiler_params=pltpu.CompilerParams(vmem_limit_bytes=EARLY_VMEM),
        name="transmission",
    )(*held)


def column_kernel(plan, counts, merged, *refs):
    n = plan.group
    waves, refs = [refs[g * n : (g + 1) * n] for g in range(len(counts))], refs[len(counts) * n :]
    slices = []
    for count in counts:
        slices.append(refs[:count])
        refs = refs[count:]
    blocks, outs = refs[0], refs[1:-6]
    field, x_high, x_low, y, held, sems = refs[-6:]
    me, step = lax.axis_index("rows"), pl.program_id(0)
    load = lambda g, case: pltpu.make_async_copy(slices[g][case], held.at[g], sems.at[g])

    @pl.when(step == 0)
    def _():
        for g, cases in enumerate(slices):
            for case in range(len(cases)):
                @pl.when(plan.guest() % len(cases) == case)
                def _(g=g, case=case):
                    load(g, case).start()

    for g in range(len(counts)):

        @pl.when(step == g)
        def _(g=g):
            load(g, 0).wait()

    rows, side = plan.rows, plan.length // RADIX
    for g in range(len(counts)):
        for jump in range(n):

            @pl.when(step == g)
            def _(g=g, jump=jump):
                base = jnp.bitwise_xor(me, jump) * rows

                @pl.loop(0, rows // STRIP)
                def _(s):
                    here = pl.ds(pl.multiple_of(s * STRIP, STRIP), STRIP)
                    t_re, t_im = held[g, jump, 0, here], held[g, jump, 1, here]
                    w_re, w_im = waves[g][jump][0, here], waves[g][jump][1, here]
                    there = pl.ds(pl.multiple_of(base + s * STRIP, STRIP), STRIP)
                    field[0, there] = w_re * t_re - w_im * t_im
                    field[1, there] = w_re * t_im + w_im * t_re

    @pl.loop(0, side // STRIP)
    def _(s):
        at = lambda b: pl.ds(pl.multiple_of(b * side + s * STRIP, STRIP), STRIP)
        here = pl.ds(pl.multiple_of(s * STRIP, STRIP), STRIP)
        for k, z in enumerate(dft8([(field[0, at(b)], field[1, at(b)]) for b in range(RADIX)], -1)):
            x_high[k, here], x_low[k, here] = split(jnp.concatenate(z, axis=1))

    @pl.loop(0, RADIX)
    def _(k):
        by_re = dot3(blocks[k, 0, 0], blocks[k, 0, 1], x_high[k], x_low[k])
        by_im = dot3(blocks[k, 1, 0], blocks[k, 1, 1], x_high[k], x_low[k])
        y[k, :, :LANES] = by_re[:, :LANES] - by_im[:, LANES:]
        y[k, :, LANES:] = by_re[:, LANES:] + by_im[:, :LANES]

    @pl.loop(0, side // STRIP)
    def _(s):
        here = pl.ds(pl.multiple_of(s * STRIP, STRIP), STRIP)
        for b, z in enumerate(dft8([(y[k, here, :LANES], y[k, here, LANES:]) for k in range(RADIX)], 1)):
            there = pl.ds(pl.multiple_of(b * side + s * STRIP, STRIP), STRIP)
            field[0, there], field[1, there] = z

    for jump in range(n):
        start = jnp.bitwise_xor(me, jump) * rows
        if jump < plan.low or merged:
            there = pl.ds(pl.multiple_of(start, rows), rows)
            out = target(plan, outs, jump)
            out[0, 0], out[0, 1] = field[0, there], field[1, there]
            continue
        count = (len(outs) - plan.low) // (n - plan.low)
        for out in outs[plan.low + (jump - plan.low) * count :][:count]:
            tall = out.shape[2]
            there = pl.ds(pl.multiple_of(start, tall), tall)
            out[0, 0], out[0, 1] = field[0, there], field[1, there]
            start += tall


def taken(array, rows, start, picks, pick):
    lead = (pl.squeezed,) * (array.ndim - 4)
    return pl.BlockSpec(lead + (picks, 2, rows, LANES), lambda g: (0,) * len(lead) + (pick(g), 0, start, 0))


def column_pass(plan, part, waves, slices, blocks):
    side = plan.length // RADIX
    picks = len(plan.parts[part])
    chunks, merged = plan.sends[part]
    flat = [array for cases in slices for array in cases]
    return pl.pallas_call(
        functools.partial(column_kernel, plan, [len(cases) for cases in slices], merged),
        grid=(picks,),
        out_shape=shapes(plan, picks, chunks, merged, 0 if merged else SPARE),
        in_specs=[taken(array, plan.rows, 0, pl.squeezed, lambda g, at=at: at) for of in waves for array, at in of]
        + [pl.BlockSpec(memory_space=pl.ANY)] * len(flat)
        + [pl.BlockSpec((RADIX, 2, 2, side, side), lambda g: (0, 0, 0, 0, 0))],
        out_specs=outputs(
            plan,
            chunks,
            merged,
            lambda rows: pl.BlockSpec((1, 2, rows, LANES), lambda g: (g, 0, 0, 0)),
            lambda rows: pl.BlockSpec((plan.low, 1, 2, rows, LANES), lambda g: (0, g, 0, 0, 0)),
            lambda rows: pl.BlockSpec((1, 2, rows, LANES), lambda g: (g, 0, 0, 0)),
        ),
        scratch_shapes=[
            pltpu.VMEM((2, plan.length, LANES), f32),
            pltpu.VMEM((RADIX, side, 2 * LANES), bf16),
            pltpu.VMEM((RADIX, side, 2 * LANES), bf16),
            pltpu.VMEM((RADIX, side, 2 * LANES), f32),
            pltpu.VMEM((picks, plan.group, 2, plan.rows, LANES), f32),
            pltpu.SemaphoreType.DMA((picks,)),
        ],
        compiler_params=pltpu.CompilerParams(vmem_limit_bytes=VMEM),
        cost_estimate=pl.CostEstimate(flops=0, bytes_accessed=1024, transcendentals=0),
        name=f"column_pass_{part}",
    )(*[array for of in waves for array, _ in of], *flat, blocks)


def row_kernel(plan, chunk, *refs):
    n = plan.group
    ins, blocks, out = refs[: len(plan.parts) * n], refs[len(plan.parts) * n], refs[-9]
    field, d, x, y, staged, in_sems, d_sem, out_sems = refs[-8:]
    me, dist = lax.axis_index("rows"), lax.axis_index("dist")
    side, tall = plan.length // RADIX, plan.chunks[chunk]
    first = sum(plan.chunks[:chunk])
    group = tall // GROUPS
    loads = [[] for _ in range(GROUPS)]
    for r in range(GROUPS):
        here = pl.ds(r * group, group)
        for part, picks in enumerate(plan.parts):
            for jump in range(n):
                array = ins[part * n + jump]
                start = r * group + (0 if array.shape[-2] == tall else first)
                array = array.at[0] if len(array.shape) > 4 else array
                for g, pick in enumerate(picks):
                    unit = plan.unit(jnp.bitwise_xor(me, jump), dist, pick)
                    sem = in_sems.at[r, len(loads[r])]
                    loads[r].append(pltpu.make_async_copy(array.at[g, :, pl.ds(start, group)], field.at[unit, :, here], sem))
    load_blocks = pltpu.make_async_copy(blocks, d, d_sem)
    load_blocks.start()
    for load in loads[0]:
        load.start()
    for of in loads[1:]:
        for load in of:
            load.start()
    wide = side // LANES

    for r in range(GROUPS):
        for load in loads[r]:
            load.wait()

        @pl.loop(0, group // ROW_STRIP)
        def _(s, r=r):
            here = pl.ds(pl.multiple_of(r * group + s * ROW_STRIP, ROW_STRIP), ROW_STRIP)
            line = lambda b, c: jnp.concatenate([field[b * wide + v, c, here] for v in range(wide)], axis=1)
            for k, z in enumerate(dft8([(line(b, 0), line(b, 1)) for b in range(RADIX)], -1)):
                for c in range(2):
                    x[k, 0, c, here], x[k, 1, c, here] = split(z[c])

    load_blocks.wait()

    for k in range(RADIX):
        back = (RADIX - k) % RADIX
        both = x[k].reshape(4 * tall, side)
        high = both[: 2 * tall]

        def by(c):
            product = jnp.dot(both, d[back, c, 0], preferred_element_type=f32)
            return product[: 2 * tall] + product[2 * tall :] + jnp.dot(high, d[back, c, 1], preferred_element_type=f32)

        by_re, by_im = by(0), by(1)
        y[k, 0] = by_re[:tall] - by_im[tall:]
        y[k, 1] = by_re[tall:] + by_im[:tall]

    stores = []
    for r in range(GROUPS):

        @pl.loop(0, group // ROW_STRIP)
        def _(s, r=r):
            here = pl.ds(pl.multiple_of(r * group + s * ROW_STRIP, ROW_STRIP), ROW_STRIP)
            for b, z in enumerate(dft8([(y[k, 0, here], y[k, 1, here]) for k in range(RADIX)], 1)):
                staged[0, here, b * side : (b + 1) * side], staged[1, here, b * side : (b + 1) * side] = z

        stores.append(
            pltpu.make_async_copy(
                staged.at[:, pl.ds(r * group, group)], out.at[0, :, pl.ds(first + r * group, group)], out_sems.at[r]
            )
        )
        stores[-1].start()
    for store in stores:
        store.wait()


def row_pass(plan, chunk, ins, blocks, result):
    side, tall = plan.length // RADIX, plan.chunks[chunk]
    operands = [array for of in ins for array in of] + [blocks]
    aliases = {}
    if result is not None:
        operands.append(result)
        aliases = {len(operands) - 1: 0}
    return pl.pallas_call(
        functools.partial(row_kernel, plan, chunk),
        out_shape=jax.ShapeDtypeStruct((1, 2, plan.rows, plan.length), f32),
        in_specs=[pl.BlockSpec(memory_space=pl.ANY)] * len(operands),
        out_specs=pl.BlockSpec(memory_space=pltpu.HBM),
        scratch_shapes=[
            pltpu.VMEM((plan.units, 2, tall, LANES), f32),
            pltpu.VMEM((RADIX, 2, 2, side, side), bf16),
            pltpu.VMEM((RADIX, 2, 2, tall, side), bf16),
            pltpu.VMEM((RADIX, 2, tall, side), f32),
            pltpu.VMEM((2, tall, plan.length), f32),
            pltpu.SemaphoreType.DMA((GROUPS, plan.units)),
            pltpu.SemaphoreType.DMA,
            pltpu.SemaphoreType.DMA((GROUPS,)),
        ],
        input_output_aliases=aliases,
        compiler_params=pltpu.CompilerParams(vmem_limit_bytes=VMEM),
        cost_estimate=pl.CostEstimate(flops=6 * MIB * 1024 * tall // plan.rows, bytes_accessed=20 * MIB * tall // plan.rows, transcendentals=0),
        name=f"row_pass_{chunk}",
    )(*operands)


def jumped(array, axis, jump):
    return lax.ppermute(array, axis, [(i, i ^ jump) for i in range(lax.axis_size(axis))])


def pick(which, cases):
    return cases[0] if len(cases) == 1 else lax.select_n(which, *cases) if len(cases) > 2 else jnp.where(which == 0, *cases)


def after(array, *others):
    return lax.optimization_barrier((array, *others))[0]


def piece_of(object_slice, place, plan):
    width = object_slice.shape[2] // plan.high
    return lax.dynamic_slice_in_dim(object_slice, place // plan.low * width, width, 2)


def owned(plan, object_slice):
    me = lax.axis_index("rows")
    blocks = [piece_of(object_slice, jnp.bitwise_xor(me, h * 2), plan) for h in range(plan.high)]
    held = [blocks[0]]
    for jump in range(1, plan.group):
        pairs = [
            (d * plan.group + (i ^ jump), d * plan.group + i)
            for d in range(plan.dists)
            for i in range(plan.group)
            if i % 2 == d % 2
        ]
        held.append(lax.ppermute(blocks[jump // 2], ("dist", "rows"), pairs))
    return held


def owners_round(plan, through, blocks, first):
    group, dists = plan.group, plan.dists
    lines = lambda to: [(d * group + i, to(d) * group + i) for d in range(dists) for i in range(group) if i % 2 == d % 2]
    both = ("dist", "rows")
    mine, last = [through], []
    for g in range(1, plan.picks):
        mine.append(lax.ppermute(mine[-1], both, lines(lambda d: (d + 2) % dists)))
    for g in range(plan.picks):
        held = after(mine[g], blocks, first, *last) if g else through
        last = [lax.ppermute(held, both, lines(lambda d: d ^ 1))]
        wait = yield [held, last[0]]
        last += wait or []


def spread(plan, through):
    me, dist = lax.axis_index("rows"), lax.axis_index("dist")
    pieces = lax.all_gather(through, "dist")
    found = []
    for g in range(plan.picks):
        first = lax.rem(dist // plan.low + (plan.picks - g), plan.picks) * plan.low
        parts = []
        for l in range(plan.low):
            block = lax.dynamic_index_in_dim(pieces, first + jnp.bitwise_xor(me % plan.low, l), keepdims=False)
            parts.append(jumped(block, "rows", l) if l else block)
        found.append([jnp.stack(parts, 1).reshape((plan.group,) + through.shape[1:])])
    return found


def sent_far(plan, outs, ahead=()):
    return [jumped(after(block, *ahead), "rows", h * plan.low) for h, block in enumerate(outs[plan.low :], 1)]


def sent_near(plan, outs):
    return [jumped(block, "rows", l) if l else block for l, block in enumerate(outs[: plan.low])]


def sent_on(plan, far, ahead=()):
    got = []
    for block in far:
        got.append(block)
        onward = after(block, *ahead)
        got += [jumped(onward[l], "rows", l) for l in range(1, plan.low)]
    return got


def body(wave, object_slice, fresnel):
    plan = Plan(wave)
    group, high, low = plan.group, plan.high, plan.low
    me = lax.axis_index("rows")

    if low == 2:
        held = owned(plan, object_slice)
    else:
        held = [piece_of(object_slice, jnp.bitwise_xor(me, h * low), plan) for h in range(high)]
        held = [jumped(block, "rows", h * low) if h else block for h, block in enumerate(held)]

    packed = pack(plan, wave)
    held[0] = after(held[0], *[block for blocks in packed for block in blocks])
    sent = [sent_near(plan, outs) + sent_on(plan, sent_far(plan, outs)) for outs in packed]
    waves = [[(array, at) for array in got] for got, picks in zip(sent, plan.batches) for at in range(len(picks))]

    through = transmission(held)
    blocks = circulant_blocks(after(fresnel, through), plan.length)
    rounds = owners_round(plan, through, blocks, sent[0][low]) if low == 2 else iter(spread(plan, through))

    gone, slices, last = [], [], len(plan.parts) - 1
    for part, picks in enumerate(plan.parts):
        while len(slices) <= picks[-1]:
            wait = [sent[-1][low], outs[0]] if low == 2 and len(slices) == 2 else None
            slices.append(rounds.send(wait) if wait else next(rounds))
        here = slice(picks[0], picks[-1] + 1)
        if part and part == last:
            gone[0] += sent_on(plan, flown, outs[:1])
            blocks = after(blocks, *gone[0], *gone[1][:low])
        outs = column_pass(plan, part, waves[here], slices[here], blocks)
        gone.append(sent_near(plan, outs))
        if part == 0:
            flown = sent_far(plan, outs, [sent[-1][j] for j in range(low, group, low)] if last else [])
        elif part < last:
            gone[-1] += [jumped(block, "rows", j) for j, block in enumerate(outs[low:], low)]
    result, count = None, len(plan.chunks)
    if not last:
        gone[0] += sent_on(plan, flown)
    for chunk in range(count):
        ins = list(gone)
        if last:
            far = [outs[low + (j - low) * count + chunk] for j in range(low, group)]
            ins[-1] = gone[-1] + [jumped(block, "rows", j) for j, block in enumerate(far, low)]
        result = row_pass(plan, chunk, ins, blocks, result)
    return result


def solution(mesh):
    return jax.shard_map(
        body,
        mesh=mesh,
        in_specs=(P("dist", None, "rows", None), P(None, "rows", "dist"), P("dist")),
        out_specs=P("dist", None, "rows", None),
        check_vma=False,
    )
```

```python
import functools
import math

import jax
import jax.numpy as jnp
import numpy as np
from jax import lax
from jax.experimental import pallas as pl
from jax.experimental.pallas import tpu as pltpu
from jax.sharding import PartitionSpec as P

f32, bf16 = jnp.float32, jnp.bfloat16
LANES = 128
RADIX = 8
STRIP = 32
ROW_STRIP = 16
GROUPS = 8
SPARE = 8
MIB = 1 << 20
VMEM = 64 * MIB - 256 * 1024
EARLY_VMEM = 56 * MIB
ROOT = math.sqrt(0.5)


def turn(z, quarter):
    re, im = z
    return ((re, im), (-im, re), (-re, -im), (im, -re))[quarter % 4]


def plus(a, b):
    return (a[0] + b[0], a[1] + b[1])


def minus(a, b):
    return (a[0] - b[0], a[1] - b[1])


def dft4(z, sign):
    even, odd = plus(z[0], z[2]), plus(z[1], z[3])
    low, high = minus(z[0], z[2]), turn(minus(z[1], z[3]), sign)
    return [plus(even, odd), plus(low, high), minus(even, odd), minus(low, high)]


def dft8(z, sign):
    even, odd = dft4(z[0::2], sign), dft4(z[1::2], sign)
    (re1, im1), (re3, im3) = odd[1], odd[3]
    odd[1] = (ROOT * (re1 - sign * im1), ROOT * (im1 + sign * re1))
    odd[2] = turn(odd[2], sign)
    odd[3] = (-ROOT * (re3 + sign * im3), ROOT * (sign * re3 - im3))
    return [plus(a, b) for a, b in zip(even, odd)] + [minus(a, b) for a, b in zip(even, odd)]


def split(value):
    high = value.astype(bf16)
    return high, (value - high.astype(f32)).astype(bf16)


def dot3(a_high, a_low, b_high, b_low):
    dot = functools.partial(jnp.dot, preferred_element_type=f32)
    return dot(a_high, b_high) + (dot(a_high, b_low) + dot(a_low, b_high))


def blocks_kernel(response, wheel, right, twist, blocks):
    half = wheel.shape[1]
    k = pl.program_id(0)
    h_re, h_im = response[0, pl.ds(k, 1)], response[1, pl.ds(k, 1)]
    w_re, w_im = wheel[0], wheel[1]
    left = jnp.concatenate((w_re * h_re - w_im * h_im, w_re * h_im + w_im * h_re), axis=1)
    both = jnp.dot(left, right[...], precision=lax.Precision.HIGHEST, preferred_element_type=f32)
    both_re, both_im = both[:, :half], both[:, half:]
    t_re, t_im = twist[0, 0], twist[0, 1]
    high, low = split(both_re * t_re - both_im * t_im)
    blocks[0, 0, 0], blocks[0, 0, 1] = high, low
    high, low = split(both_re * t_im + both_im * t_re)
    blocks[0, 1, 0], blocks[0, 1, 1] = high, low


def circulant_blocks(fresnel, length):
    side = length // RADIX
    index = np.arange(RADIX)[:, None] + RADIX * np.arange(side)[None]
    freq = np.where(index < length // 2, index, index - length).astype(np.float32) / length
    phase = (-math.pi * fresnel[0]) * (freq * freq)
    response = jnp.stack((jnp.cos(phase), jnp.sin(phase)))
    line = np.arange(side)
    angle = 2 * np.pi / side * (line[:, None] * line[None] % side)
    wheel = np.stack((np.cos(angle), np.sin(angle))).astype(np.float32)
    scale = 1.0 / (side * RADIX)
    w_re, w_im = np.cos(angle).T * scale, np.sin(angle).T * scale
    right = np.block([[w_re, -w_im], [w_im, w_re]]).astype(np.float32)
    apart = np.arange(RADIX)[:, None, None] * (line[:, None] - line[None])
    twist = np.stack((np.cos(2 * np.pi / length * apart), np.sin(2 * np.pi / length * apart)), 1).astype(np.float32)
    whole = lambda *shape: pl.BlockSpec(shape, lambda k: (0,) * len(shape))
    return pl.pallas_call(
        blocks_kernel,
        grid=(RADIX,),
        out_shape=jax.ShapeDtypeStruct((RADIX, 2, 2, side, side), bf16),
        in_specs=[
            whole(2, RADIX, side),
            whole(2, side, side),
            whole(2 * side, 2 * side),
            pl.BlockSpec((1, 2, side, side), lambda k: (k, 0, 0, 0)),
        ],
        out_specs=pl.BlockSpec((1, 2, 2, side, side), lambda k: (k, 0, 0, 0, 0)),
        compiler_params=pltpu.CompilerParams(vmem_limit_bytes=EARLY_VMEM),
        name="circulant_blocks",
    )(response, jnp.asarray(wheel), jnp.asarray(right), jnp.asarray(twist))


class Plan:
    def __init__(self, wave):
        self.group, self.dists = lax.axis_size("rows"), lax.axis_size("dist")
        self.rows, self.length = wave.shape[2], wave.shape[3]
        self.units = self.length // LANES
        self.high = min(self.units // self.dists, self.group)
        self.low = self.group // self.high
        self.picks = self.dists // self.low
        halves = self.picks == 4
        self.batches = [[0, 1], [2, 3]] if halves else [list(range(self.picks))]
        self.parts = [[0, 1], [2], [3]] if halves else [list(range(self.picks))]
        self.chunks = [self.rows // 2] * 2 if halves and self.rows // 4 >= LANES else [self.rows]
        self.sends = [([self.rows], True), ([self.rows], False), (self.chunks, False)] if halves else [([self.rows], True)]
        self.order = sorted(range(self.group), key=lambda jump: (-(jump // self.low), jump % self.low))

    def guest(self):
        return jnp.bitwise_xor(lax.axis_index("rows") % self.low, lax.axis_index("dist") % self.low)

    def unit(self, place, dist, pick):
        other = lax.rem(dist // self.low + (self.picks - pick), self.picks) * self.low + place % self.low
        return other * self.high + place // self.low


def outputs(plan, chunks, merged, near, far, direct):
    nears = [near(plan.rows) for _ in range(plan.low)]
    if merged:
        return nears + [far(plan.rows) for _ in range(plan.high - 1)]
    return nears + [direct(rows) for _ in range(plan.low, plan.group) for rows in chunks]


def shapes(plan, picks, chunks, merged, spare=0):
    shape = lambda *dims: jax.ShapeDtypeStruct(dims, f32)
    return outputs(
        plan,
        chunks,
        merged,
        lambda rows: shape(picks, 2, rows, LANES),
        lambda rows: shape(plan.low, picks, 2, rows + spare, LANES),
        lambda rows: shape(picks, 2, rows + (spare if rows == plan.rows else 0), LANES),
    )


def target(plan, outs, jump):
    high, low = jump // plan.low, jump % plan.low
    return outs[plan.low + high - 1].at[low] if high else outs[low]


def pack_kernel(plan, wave, *refs):
    outs, (staged, ins, sems) = refs[:-3], refs[-3:]
    me, dist = lax.axis_index("rows"), lax.axis_index("dist")
    size = len(outs) // len(plan.batches)
    loads, stores = [], []
    for batch, picks in enumerate(plan.batches):
        for jump in plan.order:
            for at, pick in enumerate(picks):
                slot = len(loads)
                unit = plan.unit(jnp.bitwise_xor(me, jump), dist, pick)
                start = pl.multiple_of(unit * LANES, LANES)
                out = target(plan, outs[batch * size : (batch + 1) * size], jump).at[at, :, pl.ds(0, plan.rows)]
                loads.append(pltpu.make_async_copy(wave.at[0, :, :, pl.ds(start, LANES)], staged.at[slot], ins.at[slot]))
                stores.append(pltpu.make_async_copy(staged.at[slot], out, sems.at[slot]))
    for load in loads:
        load.start()
    for load, store in zip(loads, stores):
        load.wait()
        store.start()
    for store in stores:
        store.wait()


def pack(plan, wave):
    outs = [shape for picks in plan.batches for shape in shapes(plan, len(picks), [plan.rows], True, SPARE)]
    hbm = pl.BlockSpec(memory_space=pltpu.HBM)
    outs = pl.pallas_call(
        functools.partial(pack_kernel, plan),
        out_shape=outs,
        in_specs=[hbm],
        out_specs=[hbm] * len(outs),
        scratch_shapes=[
            pltpu.VMEM((plan.units, 2, plan.rows, LANES), f32),
            pltpu.SemaphoreType.DMA((plan.units,)),
            pltpu.SemaphoreType.DMA((plan.units,)),
        ],
        compiler_params=pltpu.CompilerParams(vmem_limit_bytes=EARLY_VMEM),
        cost_estimate=pl.CostEstimate(flops=0, bytes_accessed=16 * MIB, transcendentals=0),
        name="pack",
    )(wave)
    size = len(outs) // len(plan.batches)
    return [outs[batch * size : (batch + 1) * size] for batch in range(len(plan.batches))]


def series(square, first, count):
    total = jnp.ones_like(square)
    for i in reversed(range(count)):
        total = 1.0 - square * (1.0 / ((first + 2 * i) * (first + 2 * i + 1))) * total
    return total


def transmission_kernel(*refs):
    out = refs[-1]
    for h, piece in enumerate(refs[:-1]):
        amplitude, square = jnp.exp(-piece[1]), piece[0] * piece[0]
        out[h, 0] = amplitude * series(square, 1, 7)
        out[h, 1] = amplitude * (piece[0] * series(square, 2, 7))


def transmission(held):
    rows = held[0].shape[1]
    tall = min(rows, LANES)
    return pl.pallas_call(
        transmission_kernel,
        grid=(rows // tall,),
        out_shape=jax.ShapeDtypeStruct((len(held),) + held[0].shape, f32),
        in_specs=[pl.BlockSpec((2, tall, LANES), lambda s: (0, s, 0))] * len(held),
        out_specs=pl.BlockSpec((len(held), 2, tall, LANES), lambda s: (0, 0, s, 0)),
        compiler_params=pltpu.CompilerParams(vmem_limit_bytes=EARLY_VMEM),
        name="transmission",
    )(*held)


def column_kernel(plan, counts, merged, *refs):
    n = plan.group
    waves, refs = [refs[g * n : (g + 1) * n] for g in range(len(counts))], refs[len(counts) * n :]
    slices = []
    for count in counts:
        slices.append(refs[:count])
        refs = refs[count:]
    blocks, outs = refs[0], refs[1:-6]
    field, x_high, x_low, y, held, sems = refs[-6:]
    me, step = lax.axis_index("rows"), pl.program_id(0)
    load = lambda g, case: pltpu.make_async_copy(slices[g][case], held.at[g], sems.at[g])

    @pl.when(step == 0)
    def _():
        for g, cases in enumerate(slices):
            for case in range(len(cases)):
                @pl.when(plan.guest() % len(cases) == case)
                def _(g=g, case=case):
                    load(g, case).start()

    for g in range(len(counts)):

        @pl.when(step == g)
        def _(g=g):
            load(g, 0).wait()

    rows, side = plan.rows, plan.length // RADIX
    for g in range(len(counts)):
        for jump in range(n):

            @pl.when(step == g)
            def _(g=g, jump=jump):
                base = jnp.bitwise_xor(me, jump) * rows

                @pl.loop(0, rows // STRIP)
                def _(s):
                    here = pl.ds(pl.multiple_of(s * STRIP, STRIP), STRIP)
                    t_re, t_im = held[g, jump, 0, here], held[g, jump, 1, here]
                    w_re, w_im = waves[g][jump][0, here], waves[g][jump][1, here]
                    there = pl.ds(pl.multiple_of(base + s * STRIP, STRIP), STRIP)
                    field[0, there] = w_re * t_re - w_im * t_im
                    field[1, there] = w_re * t_im + w_im * t_re

    @pl.loop(0, side // STRIP)
    def _(s):
        at = lambda b: pl.ds(pl.multiple_of(b * side + s * STRIP, STRIP), STRIP)
        here = pl.ds(pl.multiple_of(s * STRIP, STRIP), STRIP)
        for k, z in enumerate(dft8([(field[0, at(b)], field[1, at(b)]) for b in range(RADIX)], -1)):
            x_high[k, here], x_low[k, here] = split(jnp.concatenate(z, axis=1))

    @pl.loop(0, RADIX, unroll=True)
    def _(k):
        by_re = dot3(blocks[k, 0, 0], blocks[k, 0, 1], x_high[k], x_low[k])
        by_im = dot3(blocks[k, 1, 0], blocks[k, 1, 1], x_high[k], x_low[k])
        y[k, :, :LANES] = by_re[:, :LANES] - by_im[:, LANES:]
        y[k, :, LANES:] = by_re[:, LANES:] + by_im[:, :LANES]

    @pl.loop(0, side // STRIP)
    def _(s):
        here = pl.ds(pl.multiple_of(s * STRIP, STRIP), STRIP)
        for b, z in enumerate(dft8([(y[k, here, :LANES], y[k, here, LANES:]) for k in range(RADIX)], 1)):
            there = pl.ds(pl.multiple_of(b * side + s * STRIP, STRIP), STRIP)
            field[0, there], field[1, there] = z

    for jump in range(n):
        start = jnp.bitwise_xor(me, jump) * rows
        if jump < plan.low or merged:
            there = pl.ds(pl.multiple_of(start, rows), rows)
            out = target(plan, outs, jump)
            out[0, 0], out[0, 1] = field[0, there], field[1, there]
            continue
        count = (len(outs) - plan.low) // (n - plan.low)
        for out in outs[plan.low + (jump - plan.low) * count :][:count]:
            tall = out.shape[2]
            there = pl.ds(pl.multiple_of(start, tall), tall)
            out[0, 0], out[0, 1] = field[0, there], field[1, there]
            start += tall


def taken(array, rows, start, picks, pick):
    lead = (pl.squeezed,) * (array.ndim - 4)
    return pl.BlockSpec(lead + (picks, 2, rows, LANES), lambda g: (0,) * len(lead) + (pick(g), 0, start, 0))


def column_pass(plan, part, waves, slices, blocks):
    side = plan.length // RADIX
    picks = len(plan.parts[part])
    chunks, merged = plan.sends[part]
    flat = [array for cases in slices for array in cases]
    return pl.pallas_call(
        functools.partial(column_kernel, plan, [len(cases) for cases in slices], merged),
        grid=(picks,),
        out_shape=shapes(plan, picks, chunks, merged, 0 if merged else SPARE),
        in_specs=[taken(array, plan.rows, 0, pl.squeezed, lambda g, at=at: at) for of in waves for array, at in of]
        + [pl.BlockSpec(memory_space=pl.ANY)] * len(flat)
        + [pl.BlockSpec((RADIX, 2, 2, side, side), lambda g: (0, 0, 0, 0, 0))],
        out_specs=outputs(
            plan,
            chunks,
            merged,
            lambda rows: pl.BlockSpec((1, 2, rows, LANES), lambda g: (g, 0, 0, 0)),
            lambda rows: pl.BlockSpec((plan.low, 1, 2, rows, LANES), lambda g: (0, g, 0, 0, 0)),
            lambda rows: pl.BlockSpec((1, 2, rows, LANES), lambda g: (g, 0, 0, 0)),
        ),
        scratch_shapes=[
            pltpu.VMEM((2, plan.length, LANES), f32),
            pltpu.VMEM((RADIX, side, 2 * LANES), bf16),
            pltpu.VMEM((RADIX, side, 2 * LANES), bf16),
            pltpu.VMEM((RADIX, side, 2 * LANES), f32),
            pltpu.VMEM((picks, plan.group, 2, plan.rows, LANES), f32),
            pltpu.SemaphoreType.DMA((picks,)),
        ],
        compiler_params=pltpu.CompilerParams(vmem_limit_bytes=VMEM),
        cost_estimate=pl.CostEstimate(flops=0, bytes_accessed=1024, transcendentals=0),
        name=f"column_pass_{part}",
    )(*[array for of in waves for array, _ in of], *flat, blocks)


def row_kernel(plan, chunk, *refs):
    n = plan.group
    ins, blocks, out = refs[: len(plan.parts) * n], refs[len(plan.parts) * n], refs[-9]
    field, d, x, y, staged, in_sems, d_sem, out_sems = refs[-8:]
    me, dist = lax.axis_index("rows"), lax.axis_index("dist")
    side, tall = plan.length // RADIX, plan.chunks[chunk]
    first = sum(plan.chunks[:chunk])
    group = tall // GROUPS
    loads = [[] for _ in range(GROUPS)]
    for r in range(GROUPS):
        here = pl.ds(r * group, group)
        for part, picks in enumerate(plan.parts):
            for jump in range(n):
                array = ins[part * n + jump]
                start = r * group + (0 if array.shape[-2] == tall else first)
                array = array.at[0] if len(array.shape) > 4 else array
                for g, pick in enumerate(picks):
                    unit = plan.unit(jnp.bitwise_xor(me, jump), dist, pick)
                    sem = in_sems.at[r, len(loads[r])]
                    loads[r].append(pltpu.make_async_copy(array.at[g, :, pl.ds(start, group)], field.at[unit, :, here], sem))
    load_blocks = pltpu.make_async_copy(blocks, d, d_sem)
    load_blocks.start()
    for load in loads[0]:
        load.start()
    for of in loads[1:]:
        for load in of:
            load.start()
    wide = side // LANES

    for r in range(GROUPS):
        for load in loads[r]:
            load.wait()

        @pl.loop(0, group // ROW_STRIP)
        def _(s, r=r):
            here = pl.ds(pl.multiple_of(r * group + s * ROW_STRIP, ROW_STRIP), ROW_STRIP)
            line = lambda b, c: jnp.concatenate([field[b * wide + v, c, here] for v in range(wide)], axis=1)
            for k, z in enumerate(dft8([(line(b, 0), line(b, 1)) for b in range(RADIX)], -1)):
                for c in range(2):
                    x[k, 0, c, here], x[k, 1, c, here] = split(z[c])

    load_blocks.wait()

    for k in range(RADIX):
        back = (RADIX - k) % RADIX
        both = x[k].reshape(4 * tall, side)
        high = both[: 2 * tall]

        def by(c):
            product = jnp.dot(both, d[back, c, 0], preferred_element_type=f32)
            return product[: 2 * tall] + product[2 * tall :] + jnp.dot(high, d[back, c, 1], preferred_element_type=f32)

        by_re, by_im = by(0), by(1)
        y[k, 0] = by_re[:tall] - by_im[tall:]
        y[k, 1] = by_re[tall:] + by_im[:tall]

    stores = []
    for r in range(GROUPS):

        @pl.loop(0, group // ROW_STRIP)
        def _(s, r=r):
            here = pl.ds(pl.multiple_of(r * group + s * ROW_STRIP, ROW_STRIP), ROW_STRIP)
            for b, z in enumerate(dft8([(y[k, 0, here], y[k, 1, here]) for k in range(RADIX)], 1)):
                staged[0, here, b * side : (b + 1) * side], staged[1, here, b * side : (b + 1) * side] = z

        stores.append(
            pltpu.make_async_copy(
                staged.at[:, pl.ds(r * group, group)], out.at[0, :, pl.ds(first + r * group, group)], out_sems.at[r]
            )
        )
        stores[-1].start()
    for store in stores:
        store.wait()


def row_pass(plan, chunk, ins, blocks, result):
    side, tall = plan.length // RADIX, plan.chunks[chunk]
    operands = [array for of in ins for array in of] + [blocks]
    aliases = {}
    if result is not None:
        operands.append(result)
        aliases = {len(operands) - 1: 0}
    return pl.pallas_call(
        functools.partial(row_kernel, plan, chunk),
        out_shape=jax.ShapeDtypeStruct((1, 2, plan.rows, plan.length), f32),
        in_specs=[pl.BlockSpec(memory_space=pl.ANY)] * len(operands),
        out_specs=pl.BlockSpec(memory_space=pltpu.HBM),
        scratch_shapes=[
            pltpu.VMEM((plan.units, 2, tall, LANES), f32),
            pltpu.VMEM((RADIX, 2, 2, side, side), bf16),
            pltpu.VMEM((RADIX, 2, 2, tall, side), bf16),
            pltpu.VMEM((RADIX, 2, tall, side), f32),
            pltpu.VMEM((2, tall, plan.length), f32),
            pltpu.SemaphoreType.DMA((GROUPS, plan.units)),
            pltpu.SemaphoreType.DMA,
            pltpu.SemaphoreType.DMA((GROUPS,)),
        ],
        input_output_aliases=aliases,
        compiler_params=pltpu.CompilerParams(vmem_limit_bytes=VMEM),
        cost_estimate=pl.CostEstimate(flops=6 * MIB * 1024 * tall // plan.rows, bytes_accessed=20 * MIB * tall // plan.rows, transcendentals=0),
        name=f"row_pass_{chunk}",
    )(*operands)


def jumped(array, axis, jump):
    return lax.ppermute(array, axis, [(i, i ^ jump) for i in range(lax.axis_size(axis))])


def pick(which, cases):
    return cases[0] if len(cases) == 1 else lax.select_n(which, *cases) if len(cases) > 2 else jnp.where(which == 0, *cases)


def after(array, *others):
    return lax.optimization_barrier((array, *others))[0]


def piece_of(object_slice, place, plan):
    width = object_slice.shape[2] // plan.high
    return lax.dynamic_slice_in_dim(object_slice, place // plan.low * width, width, 2)


def owned(plan, object_slice):
    me = lax.axis_index("rows")
    blocks = [piece_of(object_slice, jnp.bitwise_xor(me, h * 2), plan) for h in range(plan.high)]
    held = [blocks[0]]
    for jump in range(1, plan.group):
        pairs = [
            (d * plan.group + (i ^ jump), d * plan.group + i)
            for d in range(plan.dists)
            for i in range(plan.group)
            if i % 2 == d % 2
        ]
        held.append(lax.ppermute(blocks[jump // 2], ("dist", "rows"), pairs))
    return held


def owners_round(plan, through, blocks, first):
    group, dists = plan.group, plan.dists
    lines = lambda to: [(d * group + i, to(d) * group + i) for d in range(dists) for i in range(group) if i % 2 == d % 2]
    both = ("dist", "rows")
    mine, last = [through], []
    for g in range(1, plan.picks):
        mine.append(lax.ppermute(mine[-1], both, lines(lambda d: (d + 2) % dists)))
    for g in range(plan.picks):
        held = after(mine[g], blocks, first, *last) if g else through
        last = [lax.ppermute(held, both, lines(lambda d: d ^ 1))]
        wait = yield [held, last[0]]
        last += wait or []


def spread(plan, through):
    me, dist = lax.axis_index("rows"), lax.axis_index("dist")
    pieces = lax.all_gather(through, "dist")
    found = []
    for g in range(plan.picks):
        first = lax.rem(dist // plan.low + (plan.picks - g), plan.picks) * plan.low
        parts = []
        for l in range(plan.low):
            block = lax.dynamic_index_in_dim(pieces, first + jnp.bitwise_xor(me % plan.low, l), keepdims=False)
            parts.append(jumped(block, "rows", l) if l else block)
        found.append([jnp.stack(parts, 1).reshape((plan.group,) + through.shape[1:])])
    return found


def sent_far(plan, outs, ahead=()):
    return [jumped(after(block, *ahead), "rows", h * plan.low) for h, block in enumerate(outs[plan.low :], 1)]


def sent_near(plan, outs):
    return [jumped(block, "rows", l) if l else block for l, block in enumerate(outs[: plan.low])]


def sent_on(plan, far, ahead=()):
    got = []
    for block in far:
        got.append(block)
        onward = after(block, *ahead)
        got += [jumped(onward[l], "rows", l) for l in range(1, plan.low)]
    return got


def body(wave, object_slice, fresnel):
    plan = Plan(wave)
    group, high, low = plan.group, plan.high, plan.low
    me = lax.axis_index("rows")

    if low == 2:
        held = owned(plan, object_slice)
    else:
        held = [piece_of(object_slice, jnp.bitwise_xor(me, h * low), plan) for h in range(high)]
        held = [jumped(block, "rows", h * low) if h else block for h, block in enumerate(held)]

    packed = pack(plan, wave)
    held[0] = after(held[0], *[block for blocks in packed for block in blocks])
    sent = [sent_near(plan, outs) + sent_on(plan, sent_far(plan, outs)) for outs in packed]
    waves = [[(array, at) for array in got] for got, picks in zip(sent, plan.batches) for at in range(len(picks))]

    through = transmission(held)
    blocks = circulant_blocks(after(fresnel, through), plan.length)
    rounds = owners_round(plan, through, blocks, sent[0][low]) if low == 2 else iter(spread(plan, through))

    gone, slices, last = [], [], len(plan.parts) - 1
    for part, picks in enumerate(plan.parts):
        while len(slices) <= picks[-1]:
            wait = [sent[-1][low], outs[0]] if low == 2 and len(slices) == 2 else None
            slices.append(rounds.send(wait) if wait else next(rounds))
        here = slice(picks[0], picks[-1] + 1)
        if part and part == last:
            gone[0] += sent_on(plan, flown, outs[:1])
            blocks = after(blocks, *gone[0], *gone[1][:low])
        outs = column_pass(plan, part, waves[here], slices[here], blocks)
        gone.append(sent_near(plan, outs))
        if part == 0:
            flown = sent_far(plan, outs, [sent[-1][j] for j in range(low, group, low)] if last else [])
        elif part < last:
            gone[-1] += [jumped(block, "rows", j) for j, block in enumerate(outs[low:], low)]
    result, count = None, len(plan.chunks)
    if not last:
        gone[0] += sent_on(plan, flown)
    for chunk in range(count):
        ins = list(gone)
        if last:
            far = [outs[low + (j - low) * count + chunk] for j in range(low, group)]
            ins[-1] = gone[-1] + [jumped(block, "rows", j) for j, block in enumerate(far, low)]
        result = row_pass(plan, chunk, ins, blocks, result)
    return result


def solution(mesh):
    return jax.shard_map(
        body,
        mesh=mesh,
        in_specs=(P("dist", None, "rows", None), P(None, "rows", "dist"), P("dist")),
        out_specs=P("dist", None, "rows", None),
        check_vma=False,
    )
```
